256 devices in a mesh: gx: 16 (over z_hi, y), gy: 8 (over x, core), sa: 2 (over z_lo).
Axes of the slice: x: 4, y: 4, z: 8 (z_hi: 4, z_lo: 2; z = z_hi * 2 + z_lo), core: 2. Of those that a mesh axis runs over, the one named last changes fastest.
Arguments:
- moments: bfloat16 [2, 16, 16, 128, 1024], P('sa', None, None, 'gx', 'gy'), may hold values from -6 to 6
- speed_x: bfloat16 [2, 16, 128, 1024], P('sa', None, 'gx', 'gy'), may hold values from 0.19921875 to 1.1953125
- flag_x: int32 [2, 16, 128, 1024], P('sa', None, 'gx', 'gy'), may hold values 0 or 1
- speed_y: bfloat16 [2, 16, 128, 1024], P('sa', None, 'gx', 'gy'), may hold values from 0.19921875 to 1.1953125
- flag_y: int32 [2, 16, 128, 1024], P('sa', None, 'gx', 'gy'), may hold values 0 or 1
- w_in: float32 [16, 64], replicated, may hold values from -1.5 to 1.5
- b_in: float32 [64], replicated, may hold values from -3 to 3
- w_mid: float32 [64, 64], replicated, may hold values from -0.75 to 0.75
- b_mid: float32 [64], replicated, may hold values from -3 to 3
- w_out: float32 [64, 16], replicated, may hold values from -0.75 to 0.75
- b_out: float32 [16], replicated, may hold values from -4 to 4
- final_cot: float32 [2, 16, 16, 128, 1024], P('sa', None, None, 'gx', 'gy'), may hold values from -24 to 31
Outputs:
- grad_moments: float32 [2, 16, 16, 128, 1024], P('sa', None, None, 'gx', 'gy')
- grad_w_in: float32 [16, 64], replicated
- grad_b_in: float32 [64], replicated
- grad_w_mid: float32 [64, 64], replicated
- grad_b_mid: float32 [64], replicated
- grad_w_out: float32 [64, 16], replicated
- grad_b_out: float32 [16], replicated
The draws below stay inside these ranges and needn't reach their ends.
All inputs are finite; a program needn't handle non-finite values. No bound on the sum of `flag_x` or of `flag_y` on one device may be relied on, other than what follows from the above.
Results may differ from the reference program's by a relative error of at most 0.0025.
Values may be sent and summed in bfloat16 or wider, within the bound.
No kernel may reach another device: no remote copies, remote signals or barrier semaphores. Data moves between devices by JAX's collectives and lax.ppermute only.
A program may use at most 128 MiB of HBM per device.

```python
import jax
import jax.numpy as jnp
from jax import lax

M = 16
H = 64
NZ = 16
S = 2
NX = 128
NY = 1024
CELLS = 4194304


def draw_final_cot(key, part):
    form = (S, M, NZ, NX, NY)
    along_x = jnp.arange(NX, dtype=jnp.float32) / max(NX - 1, 1)
    along_y = jnp.arange(NY, dtype=jnp.float32) / max(NY - 1, 1)
    samples = jnp.arange(S, dtype=jnp.float32) / max(S - 1, 1)
    scale_field = 0.25 * (1.0 + 2.0 * samples)[:, None, None, None, None] * (1.0 + 2.0 * along_x)[None, None, None, :, None] * (1.0 + 2.0 * along_y)[None, None, None, None, :]
    noise = jnp.clip(jax.random.normal(key, form, jnp.float32), -4.0, 4.0)
    common = 0.5
    return (scale_field * (common + noise)).astype(jnp.float32)


def with_ends(entries, key, least, high):
    dims = entries.shape
    spot = [jax.random.randint(jax.random.fold_in(key, axis), (), 0, dims[axis]) for axis in range(len(dims))]
    entries = entries.at[tuple(spot)].set(least)
    longest = dims.index(max(dims))
    spot[longest] = (spot[longest] + 1) % dims[longest]
    return entries.at[tuple(spot)].set(high)


def levels(rng, extent, shards, low, top_value):
    gain = 1.0
    for dim, parts in shards:
        draws = jax.random.uniform(jax.random.fold_in(jax.random.fold_in(rng, 6), dim), (parts,), jnp.float32, low / len(shards), top_value / len(shards))
        gain = gain * jnp.repeat(jnp.exp(draws), extent[dim] // parts).reshape((-1,) + (1,) * (len(extent) - 1 - dim))
    return gain


def bell_draw(rng, shape, deviation, reach, cuts=(), held_as=jnp.bfloat16):
    values = jax.random.normal(rng, shape, jnp.float32) * deviation
    if len(cuts) > 0:
        values = levels(rng, shape, cuts, -0.22, 0.18) * values
    return jnp.clip(values, min=-reach, max=reach).astype(held_as)


def setup_inputs(seed: int = 0) -> dict:
    streams_of = jax.random.split(jax.random.key(seed), 13)
    moments = bell_draw(streams_of[0], (S, M, NZ, NX, NY), 1.0, 6.0, ((0, 2), (3, 16), (4, 8)))
    speed_x = jnp.clip(0.19921875 + 0.99609375 * jax.random.uniform(streams_of[1], (S, NZ, NX, NY), jnp.float32) ** levels(streams_of[1], (S, NZ, NX, NY), ((0, 2), (2, 16), (3, 8)), -0.2, 0.2), 0.19921875, 1.1953125).astype(jnp.bfloat16)
    flag_x = with_ends((jax.random.randint(streams_of[2], (S, NZ, NX, NY), 0, 2) < 1).astype(jnp.int32), jax.random.fold_in(streams_of[2], 1), 0, 1)
    speed_y = jnp.clip(0.19921875 + 0.99609375 * jax.random.uniform(streams_of[3], (S, NZ, NX, NY), jnp.float32) ** levels(streams_of[3], (S, NZ, NX, NY), ((0, 2), (2, 16), (3, 8)), -0.2, 0.2), 0.19921875, 1.1953125).astype(jnp.bfloat16)
    flag_y = with_ends((jax.random.randint(streams_of[4], (S, NZ, NX, NY), 0, 2) < 1).astype(jnp.int32), jax.random.fold_in(streams_of[4], 1), 0, 1)
    w_in = bell_draw(streams_of[5], (M, H), M ** -0.5, 1.5, (), jnp.float32)
    b_in = bell_draw(streams_of[6], (H,), 0.5, 3.0, (), jnp.float32)
    w_mid = bell_draw(streams_of[7], (H, H), H ** -0.5, 0.75, (), jnp.float32)
    b_mid = bell_draw(streams_of[8], (H,), 0.5, 3.0, (), jnp.float32)
    w_out = bell_draw(streams_of[9], (H, M), H ** -0.5, 0.75, (), jnp.float32)
    b_out = bell_draw(streams_of[10], (M,), 1.0, 4.0, (), jnp.float32)
    final_cot = draw_final_cot(jax.random.fold_in(streams_of[12], 71), 0)
    return dict(moments=moments, speed_x=speed_x, flag_x=flag_x, speed_y=speed_y, flag_y=flag_y, w_in=w_in, b_in=b_in, w_mid=w_mid, b_mid=b_mid, w_out=w_out, b_out=b_out, final_cot=final_cot)


step_dt = 0.25
highest = lax.Precision.HIGHEST


def shift_prev(value, axis):
    widths = [(0, 0)] * value.ndim
    widths[axis] = (1, 0)
    return lax.slice_in_dim(jnp.pad(value, widths), 0, value.shape[axis], axis=axis)


def shift_next(value, axis):
    widths = [(0, 0)] * value.ndim
    widths[axis] = (0, 1)
    return lax.slice_in_dim(jnp.pad(value, widths), 1, value.shape[axis] + 1, axis=axis)


def upwind(speed, flag):
    weight = flag.astype(jnp.float32)
    speed = speed.astype(jnp.float32)
    return speed * weight, speed * (1.0 - weight)


def advect(state, push_x, pull_x, push_y, pull_y):
    flux_x = push_x * state - pull_x * shift_next(state, 2)
    flux_y = push_y * state - pull_y * shift_next(state, 3)
    return flux_x - shift_prev(flux_x, 2) + flux_y - shift_prev(flux_y, 3)


def advect_adjoint(adjoint, push_x, pull_x, push_y, pull_y):
    result = push_x * (adjoint - shift_next(adjoint, 2)) + shift_prev(pull_x, 1) * (adjoint - shift_prev(adjoint, 2))
    return result + push_y * (adjoint - shift_next(adjoint, 3)) + shift_prev(pull_y, 2) * (adjoint - shift_prev(adjoint, 3))


def plane_rates(cells, weights):
    w_in, b_in, w_mid, b_mid, w_out, b_out = weights
    hidden_one = jnp.tanh(jnp.dot(w_in.T, cells, precision=highest) + b_in[:, None])
    hidden_two = jnp.tanh(jnp.dot(w_mid.T, hidden_one, precision=highest) + b_mid[:, None])
    return jnp.dot(w_out.T, hidden_two, precision=highest) + b_out[:, None]


def plane_adjoint(cells, adjoint_piece, weights):
    w_in, b_in, w_mid, b_mid, w_out, b_out = weights
    hidden_one = jnp.tanh(jnp.dot(w_in.T, cells, precision=highest) + b_in[:, None])
    hidden_two = jnp.tanh(jnp.dot(w_mid.T, hidden_one, precision=highest) + b_mid[:, None])
    grad_rate = step_dt * adjoint_piece
    grad_two = jnp.dot(w_out, grad_rate, precision=highest) * (1.0 - hidden_two * hidden_two)
    grad_one = jnp.dot(w_mid, grad_two, precision=highest) * (1.0 - hidden_one * hidden_one)
    grad_cells = jnp.dot(w_in, grad_one, precision=highest)
    grads = (jnp.einsum("mp,hp->mh", cells, grad_one, precision=highest), jnp.sum(grad_one, 1),
             jnp.einsum("gp,hp->gh", hidden_one, grad_two, precision=highest), jnp.sum(grad_two, 1),
             jnp.einsum("hp,mp->hm", hidden_two, grad_rate, precision=highest), jnp.sum(grad_rate, 1))
    return grad_cells, grads


def rates(state, weights):
    planes = jnp.moveaxis(state, 1, 0)

    def single(plane):
        form = plane.shape
        return plane_rates(plane.reshape(form[0], -1), weights).reshape(form)

    return jnp.moveaxis(lax.map(single, planes), 0, 1)


def mlp_adjoint(state, adjoint, weights):
    planes = jnp.moveaxis(state, 1, 0)
    adjoint_planes = jnp.moveaxis(adjoint, 1, 0)

    def single(pair):
        plane, adjoint_plane = pair
        form = plane.shape
        grad_cells, grads = plane_adjoint(plane.reshape(form[0], -1), adjoint_plane.reshape(form[0], -1), weights)
        return grad_cells.reshape(form), grads

    grad_planes, grads = lax.map(single, (planes, adjoint_planes))
    return jnp.moveaxis(grad_planes, 0, 1), tuple(jnp.sum(item, 0) for item in grads)


def reference(moments, speed_x, flag_x, speed_y, flag_y, w_in, b_in, w_mid, b_mid, w_out, b_out, final_cot):
    weights = (w_in, b_in, w_mid, b_mid, w_out, b_out)
    totals = [jnp.zeros_like(item) for item in weights]
    results = []
    for sample in range(S):
        push_x, pull_x = upwind(speed_x[sample], flag_x[sample])
        push_y, pull_y = upwind(speed_y[sample], flag_y[sample])
        state_zero = moments[sample].astype(jnp.float32)
        state_one = state_zero + step_dt * (rates(state_zero, weights) - advect(state_zero, push_x, pull_x, push_y, pull_y))
        adjoint = final_cot[sample]
        for state in (state_one, state_zero):
            grad_state, grads = mlp_adjoint(state, adjoint, weights)
            totals = [first + second for first, second in zip(totals, grads)]
            adjoint = adjoint + grad_state - step_dt * advect_adjoint(adjoint, push_x, pull_x, push_y, pull_y)
        results.append(adjoint)
    grad_moments = jnp.stack(results, 0)
    scaled = [item / CELLS for item in totals]
    return (grad_moments, scaled[0], scaled[1], scaled[2], scaled[3], scaled[4], scaled[5])
```

```python
import jax
import jax.numpy as jnp
from jax import lax
from jax.experimental import pallas as pl
from jax.experimental.pallas import tpu as pltpu
from jax.sharding import Mesh, PartitionSpec as P

f32 = jnp.float32
bf16 = jnp.bfloat16

NN = (((1,), (0,)), ((), ()))
NT = (((1,), (1,)), ((), ()))
TN = (((0,), (0,)), ((), ()))


def mm(a, b, dims=NN):
    return lax.dot_general(a, b, dims, preferred_element_type=f32)


def split(value):
    high = value.astype(bf16)
    return high, (value - high.astype(f32)).astype(bf16)


def iota(shape, dim):
    return lax.broadcasted_iota(jnp.int32, shape, dim)


def edge_picker(rows, length):
    row, lane = iota((2 * rows, length), 0), iota((2 * rows, length), 1)
    spot = jnp.where(row < rows, row * 128 + 127, (row - rows) * 128)
    return jnp.where(lane == spot, 1.0, 0.0).astype(bf16)


def pack_kernel(
    mom, cot, sx, fx, sy, fy, s0, v0, x_up, x_down, y_up, y_down, mom_wide, edge_wide
):
    mom_wide[...] = mom[...].astype(f32)
    edge_wide[0:128, :] = sx[...].astype(f32)
    edge_wide[128:256, :] = fx[...].astype(f32)

    def plane(z, carry):
        rows = pl.ds(pl.multiple_of(z * 16, 16), 16)
        rows_cot = pl.ds(pl.multiple_of(256 + z * 16, 16), 16)
        for x in range(8):
            tile = mom_wide[pl.ds(z * 8 + x, 16, stride=128), :].astype(bf16)
            other = cot[pl.ds(z * 8 + x, 16, stride=128), :]
            s0[rows, x * 128 : x * 128 + 128] = tile
            v0[rows, x * 128 : x * 128 + 128] = other
            if x == 7:
                x_up[rows, :] = tile
                x_up[rows_cot, :] = other.astype(bf16)
            if x == 0:
                x_down[rows, :] = tile
                x_down[rows_cot, :] = other.astype(bf16)
        return carry

    lax.fori_loop(0, 16, plane, 0)
    x_up[512:528, :] = edge_wide[pl.ds(7, 16, stride=8), :].astype(bf16)
    x_up[528:544, :] = edge_wide[pl.ds(128 + 7, 16, stride=8), :].astype(bf16)
    pick = edge_picker(8, 1024)
    ends = mm(pick, s0[...], NT)
    ends_cot = mm(pick, v0[...].astype(bf16), NT)
    y_up[:, 0:256] = ends[0:8]
    y_up[:, 256:512] = ends_cot[0:8]
    y_down[:, 0:256] = ends[8:16]
    y_down[:, 256:512] = ends_cot[8:16]
    last = jnp.where(iota((8, 128), 1) == 127, 1.0, 0.0).astype(bf16)
    y_up[:, 512:640] = mm(last, sy[...], NT)
    y_up[:, 640:768] = mm(last, fy[...].astype(f32).astype(bf16), NT)


def stacked(matrix):
    high, low = split(matrix)
    high, low = high.astype(f32), low.astype(f32)
    return jnp.concatenate([high, high, low], 0)


def bias_rows(bias):
    first = bias.astype(bf16).astype(f32)
    rest = bias - first
    second = rest.astype(bf16).astype(f32)
    third = rest - second
    row = iota((16, bias.shape[1]), 0)
    return jnp.where(row == 0, first, jnp.where(row == 1, second, jnp.where(row == 2, third, 0.0)))


def turned(matrix):
    return matrix.T.astype(bf16)


def three(pair):
    return [pair[0], pair[1], pair[0]]


def main_kernel(
    s0, v0, sx, fx, sy, fy, x_prev, x_next, y_prev, y_next,
    w_in, b_in, w_mid, b_mid, w_out, b_out,
    part, edge_coefs, x_up, x_down, y_up, y_down, sums,
    coefs, moment_ends, cot_ends, v1_held, total,
):
    flag = fx[...].astype(f32) * 0.25
    speed = sx[...].astype(f32)
    push_x, pull_x = speed * flag, speed * (0.25 - flag)
    flag = fy[...].astype(f32) * 0.25
    speed = sy[...].astype(f32)
    push_y, pull_y = speed * flag, speed * (0.25 - flag)
    row, lane = iota((128, 128), 0), iota((128, 128), 1)
    speed_prev = x_prev[512:528, :].astype(f32)
    flag_prev = x_prev[528:544, :].astype(f32) * 0.25
    wide = lambda item: jnp.broadcast_to(item[:, None, :], (16, 8, 128)).reshape(128, 128)
    first_row = lax.rem(row, 8) == 0
    pushed_x = jnp.where(first_row, wide(speed_prev * flag_prev), pltpu.roll(push_x, 1, 0))
    pulled_x = jnp.where(first_row, wide(speed_prev * (0.25 - flag_prev)), pltpu.roll(pull_x, 1, 0))
    place = jnp.where((iota((8, 128), 0) == 0) & (iota((8, 128), 1) == 0), 1.0, 0.0).astype(bf16)
    speed_prev = mm(y_prev[:, 512:640].astype(bf16), place, TN)
    flag_prev = mm(y_prev[:, 640:768].astype(bf16), place, TN) * 0.25
    pushed_y = jnp.where(lane == 0, speed_prev * flag_prev, pltpu.roll(push_y, 1, 1))
    pulled_y = jnp.where(lane == 0, speed_prev * (0.25 - flag_prev), pltpu.roll(pull_y, 1, 1))
    keep = push_x + pulled_x + push_y + pulled_y
    for index, item in enumerate(
        (keep, pull_x, pushed_x, pull_y, pushed_y, push_x, pulled_x, push_y, pulled_y)
    ):
        coefs[index * 128 : index * 128 + 128, :] = item
    for index, item in enumerate((push_x, pulled_x, push_y, pulled_y)):
        edge_coefs[index * 128 : index * 128 + 128, :] = item

    pick = edge_picker(8, 1024)
    ends = jnp.concatenate([y_next[...], y_prev[:, 0:512]], 0).astype(bf16)
    moment_ends[...] = mm(ends[:, 0:256], pick, TN)
    cot_ends[...] = mm(ends[:, 256:512], pick, TN)

    w_in_, w_mid_, w_out_ = w_in[...], w_mid[...], w_out[...]
    in_high, in_low = split(w_in_)
    in_high, in_low = in_high.astype(f32), in_low.astype(f32)
    go_in0 = turned(jnp.concatenate([in_high, in_low, bias_rows(b_in[...])], 0))
    go_in1 = turned(jnp.concatenate([in_high, in_high, in_low, bias_rows(b_in[...])], 0))
    go_mid = turned(jnp.concatenate([stacked(w_mid_), bias_rows(b_mid[...])], 0))
    go_out = turned(jnp.concatenate([stacked(w_out_ * 0.25), bias_rows(b_out[...] * 0.25)], 0))
    back_out = turned(stacked((w_out_ * 0.25).T))
    back_mid = turned(stacked(w_mid_.T))
    back_in = turned(stacked(w_in_.T))
    ones = jnp.full((16, 1024), 1.0, bf16)
    zeros = jnp.zeros((16, 1024), bf16)
    total[...] = jnp.zeros_like(total)
    end_lane = iota((16, 128), 1)

    def stencil(tiles, before, after, ends, z, first):
        around = [before] + tiles + [after]
        results = []
        for x in range(8):
            c = [
                coefs[pl.ds(k * 128 + z * 8 + x, 1), :] for k in (0, first, first + 1, first + 2, first + 3)
            ]
            here = around[x + 1]
            value = c[0] * here
            if around[x + 2] is not None:
                value = value - c[1] * around[x + 2]
            if around[x] is not None:
                value = value - c[2] * around[x]
            right, left = pltpu.roll(here, 127, 1), pltpu.roll(here, 1, 1)
            if ends is None:
                end = 0.0
            else:
                end = ends[x]
            right = jnp.where(end_lane == 127, end, right)
            left = jnp.where(end_lane == 0, end, left)
            value = value - c[3] * right - c[4] * left
            results.append(value)
        return results

    def tiles_of(value):
        return [value[:, x * 128 : x * 128 + 128] for x in range(8)]

    def join(tiles):
        return jnp.concatenate(tiles, 1)

    def cat(items):
        return jnp.concatenate(items, 0)

    def layers(lead, inputs):
        one = jnp.tanh(mm(lead, cat(inputs)))
        one_pair = split(one)
        two = jnp.tanh(mm(go_mid, cat(three(one_pair) + [ones])))
        return one, one_pair, two, split(two)

    def backward(state_pair, one, one_pair, two, two_pair, adjoint):
        adjoint_pair = split(adjoint)
        grad_two = mm(back_out, cat(three(adjoint_pair))) * (1.0 - two * two)
        two_grad_pair = split(grad_two)
        grad_one = mm(back_mid, cat(three(two_grad_pair))) * (1.0 - one * one)
        one_grad_pair = split(grad_one)
        grad_cells = mm(back_in, cat(three(one_grad_pair)))
        left_high = cat([state_pair[0], one_pair[0], adjoint_pair[0], ones])
        left_low = cat([state_pair[1], one_pair[1], adjoint_pair[1], zeros])
        right_high = cat([two_grad_pair[0], one_grad_pair[0], two_pair[0], ones])
        right_low = cat([two_grad_pair[1], one_grad_pair[1], two_pair[1], zeros])
        total[:, 0:208] += mm(left_high, right_high, NT) + (
            mm(left_high, right_low, NT) + mm(left_low, right_high, NT)
        )
        return grad_cells

    def plane(z, carry):
        start = pl.multiple_of(z * 16, 16)
        rows = pl.ds(start, 16)
        rows_cot = pl.ds(pl.multiple_of(256 + z * 16, 16), 16)
        state_zero = s0[rows, :]
        one, one_pair, two, two_pair = layers(go_in0, [state_zero, state_zero, ones])
        rate = mm(go_out, cat(three(two_pair) + [ones]))
        wide_state = state_zero.astype(f32)
        moved = stencil(
            tiles_of(wide_state), x_prev[rows, :].astype(f32), x_next[rows, :].astype(f32),
            tiles_of(moment_ends[rows, :]), z, 1,
        )
        state_one = wide_state + rate - join(moved)
        adjoint = v0[rows, :]
        state_pair = split(state_one)
        saved = layers(go_in1, three(state_pair) + [ones])
        grad_cells = backward(state_pair, *saved, adjoint)
        moved = stencil(
            tiles_of(adjoint), x_prev[rows_cot, :].astype(f32), x_next[rows_cot, :].astype(f32),
            tiles_of(cot_ends[rows, :]), z, 5,
        )
        adjoint = adjoint + grad_cells - join(moved)
        v1_held[rows, :] = adjoint.astype(bf16)
        x_up[rows, :] = adjoint[:, 896:1024].astype(bf16)
        x_down[rows, :] = adjoint[:, 0:128].astype(bf16)
        grad_cells = backward((state_zero, zeros), one, one_pair, two, two_pair, adjoint)
        moved = stencil(tiles_of(adjoint), None, None, None, z, 5)
        part[rows, :] = adjoint + grad_cells - join(moved)
        return carry

    lax.fori_loop(0, 16, plane, 0)
    ends = mm(pick, v1_held[...], NT)
    y_up[...] = ends[0:8]
    y_down[...] = ends[8:16]
    first = total[:, 0:128]
    second = total[:, 128:256]
    turn = lambda item: pltpu.roll(item, 64, 1)
    rest = jnp.concatenate(
        [first[0:16], turn(second[80:96]), first[96:104], turn(first[96:104]), second[80:96]], 0
    )
    sums[...] = jnp.where(iota((64, 128), 1) < 64, first[16:80], rest)


def finish_kernel(part, edge_coefs, x_prev, x_next, y_prev, y_next, out, ends_held):
    pick = edge_picker(8, 1024)
    ends = jnp.concatenate([y_next[...], y_prev[...]], 0).astype(bf16)
    ends_held[...] = mm(ends, pick, TN)
    end_lane = iota((1, 128), 1)

    def plane(z, carry):
        start = pl.multiple_of(z * 16, 16)
        rows = pl.ds(start, 16)
        for x in range(8):
            c = [edge_coefs[pl.ds(k * 128 + z * 8 + x, 1), :] for k in range(4)]
            value = part[rows, x * 128 : x * 128 + 128]
            weight = jnp.where(end_lane == 127, c[2], jnp.where(end_lane == 0, c[3], 0.0))
            value = value + weight * ends_held[rows, x * 128 : x * 128 + 128]
            if x == 7:
                value = value + c[0] * x_next[rows, :].astype(f32)
            if x == 0:
                value = value + c[1] * x_prev[rows, :].astype(f32)
            out[pl.ds(z * 8 + x, 16, stride=128), :] = value
        return carry

    lax.fori_loop(0, 16, plane, 0)


def weights_kernel(scale, mine, other, d_in, d_b_in, d_mid, d_b_mid, d_out, d_b_out):
    value = (mine[...] + other[...]) * scale
    moved = pltpu.roll(value, 64, 1)
    d_mid[...] = value[:, 0:64]
    d_in[...] = moved[0:16, 0:64]
    d_b_in[...] = moved[32:33, 0:64]
    d_b_mid[...] = moved[40:41, 0:64]
    d_out[...] = (moved[16:32, 0:64] * 0.25).T
    d_b_out[...] = (moved[48:64, :] * 0.25).T[0:1, :]


def shifted(block, axis, distance, count):
    route = [(i, i + distance) for i in range(count) if 0 <= i + distance < count]
    return lax.ppermute(block, axis, route)


def pairs(value, axis, links):
    return lax.ppermute(value, axis, [(a, b) for a, b in links] + [(b, a) for a, b in links])


def solution(mesh):
    parts = Mesh(mesh.devices.reshape(4, 4, 4, 2, 2), ("zh", "y", "x", "c", "zl"))
    gx, gy, sa = ("zh", "y"), ("x", "c"), "zl"
    ring = ("zh", "zl")
    wide = P(sa, None, None, gx, gy)
    flat = P(sa, None, gx, gy)
    cells = 4194304
    limit = pltpu.CompilerParams(vmem_limit_bytes=40 * 1024 * 1024)

    def local(moments, speed_x, flag_x, speed_y, flag_y, w_in, b_in, w_mid, b_mid, w_out, b_out, final_cot):
        mom = moments.reshape(2048, 128)
        cot = final_cot.reshape(2048, 128)
        sx, fx, sy, fy = (item.reshape(128, 128) for item in (speed_x, flag_x, speed_y, flag_y))
        shape = jax.ShapeDtypeStruct
        s0, v0, x_up, x_down, y_up, y_down = pl.pallas_call(
            pack_kernel,
            out_shape=(
                shape((256, 1024), bf16), shape((256, 1024), f32),
                shape((544, 128), bf16), shape((512, 128), bf16),
                shape((8, 768), f32), shape((8, 512), f32),
            ),
            scratch_shapes=[pltpu.VMEM((2048, 128), f32), pltpu.VMEM((256, 128), f32)],
            compiler_params=limit,
            name="pack",
        )(mom, cot, sx, fx, sy, fy)
        x_prev = shifted(x_up, gx, 1, 16)
        x_next = shifted(x_down, gx, -1, 16)
        y_prev = shifted(y_up, gy, 1, 8)
        y_next = shifted(y_down, gy, -1, 8)
        part, edge_coefs, x_up, x_down, y_up, y_down, sums = pl.pallas_call(
            main_kernel,
            out_shape=(
                shape((256, 1024), f32), shape((512, 128), f32),
                shape((256, 128), bf16), shape((256, 128), bf16),
                shape((8, 256), f32), shape((8, 256), f32), shape((64, 128), f32),
            ),
            scratch_shapes=[
                pltpu.VMEM((9 * 128, 128), f32), pltpu.VMEM((256, 1024), f32),
                pltpu.VMEM((256, 1024), f32), pltpu.VMEM((256, 1024), bf16),
                pltpu.VMEM((112, 256), f32),
            ],
            compiler_params=limit,
            name="network",
        )(
            s0, v0, sx, fx, sy, fy, x_prev, x_next, y_prev, y_next,
            w_in, b_in.reshape(1, 64), w_mid, b_mid.reshape(1, 64), w_out, b_out.reshape(1, 16),
        )
        x_prev = shifted(x_up, gx, 1, 16)
        x_next = shifted(x_down, gx, -1, 16)
        y_prev = shifted(y_up, gy, 1, 8)
        y_next = shifted(y_down, gy, -1, 8)
        out = pl.pallas_call(
            finish_kernel,
            out_shape=shape((2048, 128), f32),
            scratch_shapes=[pltpu.VMEM((256, 1024), f32)],
            compiler_params=limit,
            name="finish",
        )(part, edge_coefs, x_prev, x_next, y_prev, y_next)

        for axis, links in (
            ("c", [(0, 1)]),
            ("x", [(0, 1), (2, 3)]),
            ("x", [(0, 3), (1, 2)]),
            ("y", [(0, 1), (2, 3)]),
            ("y", [(0, 3), (1, 2)]),
            (ring, [(0, 1), (2, 3), (4, 5), (6, 7)]),
            (ring, [(1, 2), (3, 4), (5, 6), (7, 0)]),
        ):
            sums = sums + pairs(sums, axis, links)
        other = pairs(sums, ring, [(0, 3), (1, 6), (2, 5), (4, 7)])
        grads = pl.pallas_call(
            lambda *refs: weights_kernel(1.0 / cells, *refs),
            out_shape=(
                shape((16, 64), f32), shape((1, 64), f32), shape((64, 64), f32),
                shape((1, 64), f32), shape((64, 16), f32), shape((1, 16), f32),
            ),
            name="weights",
        )(sums, other)
        d_in, d_b_in, d_mid, d_b_mid, d_out, d_b_out = grads
        return (
            out.reshape(final_cot.shape), d_in, d_b_in.reshape(64), d_mid, d_b_mid.reshape(64),
            d_out, d_b_out.reshape(16),
        )

    return jax.shard_map(
        local,
        mesh=parts,
        in_specs=(wide, flat, flat, flat, flat, P(), P(), P(), P(), P(), P(), wide),
        out_specs=(wide, P(), P(), P(), P(), P(), P()),
        check_vma=False,
    )
```

```python
import jax
import jax.numpy as jnp
from jax import lax
from jax.experimental import pallas as pl
from jax.experimental.pallas import tpu as pltpu
from jax.sharding import Mesh, PartitionSpec as P

f32 = jnp.float32
bf16 = jnp.bfloat16

NN = (((1,), (0,)), ((), ()))
NT = (((1,), (1,)), ((), ()))
TN = (((0,), (0,)), ((), ()))
PLANES = 4
PACK = 56


def mm(a, b, dims=NN):
    return lax.dot_general(a, b, dims, preferred_element_type=f32)


def split(value):
    high = value.astype(bf16)
    return high, (value - high.astype(f32)).astype(bf16)


def iota(shape, dim):
    return lax.broadcasted_iota(jnp.int32, shape, dim)


def edge_picker(rows, length):
    row, lane = iota((2 * rows, length), 0), iota((2 * rows, length), 1)
    spot = jnp.where(row < rows, row * 128 + 127, (row - rows) * 128)
    return jnp.where(lane == spot, 1.0, 0.0).astype(bf16)


def pack_kernel(
    cot_far, mom_far, sx_far, fx_far, sy_far, fy_far,
    w_in_far, b_in_far, w_mid_far, b_mid_far, w_out_far, b_out_far,
    s0, v0, speeds, weights, x_even, x_odd, y_even, y_odd,
    cot, mom, sx, fx, sy, fy, w_in, b_in, w_mid, b_mid, w_out, b_out,
    mom_wide, x_ends, y_ends, sems,
):
    copies = [
        pltpu.make_async_copy(far, near, sems.at[i])
        for i, (far, near) in enumerate(
            (
                (cot_far, cot), (mom_far, mom), (sx_far, sx), (fx_far, fx), (sy_far, sy), (fy_far, fy),
                (w_in_far, w_in), (b_in_far, b_in), (w_mid_far, w_mid),
                (b_mid_far, b_mid), (w_out_far, w_out), (b_out_far, b_out),
            )
        )
    ]
    for copy in copies:
        copy.start()
    for copy in copies[1:]:
        copy.wait()
    mom_wide[...] = mom[...].astype(f32)
    for index, ref in enumerate((sx, fx, sy, fy)):
        speeds[index * 128 : index * 128 + 128, :] = ref[...].astype(f32)
    weights[...] = jnp.zeros((128, 128), f32)
    weights[0:64, 0:64] = w_mid[...]
    weights[64:80, 0:64] = w_in[...]
    weights[80:96, 0:64] = w_out[...]
    weights[96:97, 0:64] = b_in[...]
    weights[104:105, 0:64] = b_mid[...]
    weights[112:113, 0:16] = b_out[...]
    copies[0].wait()

    def plane(z, carry):
        rows = pl.ds(pl.multiple_of(z * 16, 16), 16)
        rows_cot = pl.ds(pl.multiple_of(256 + z * 16, 16), 16)
        for x in range(8):
            tile = mom_wide[pl.ds(z * 8 + x, 16, stride=128), :].astype(bf16)
            other = cot[pl.ds(z * 8 + x, 16, stride=128), :]
            s0[rows, x * 128 : x * 128 + 128] = tile
            v0[rows, x * 128 : x * 128 + 128] = other
            if x in (0, 7):
                side = 0 if x == 7 else 1
                x_ends[side, rows, :] = tile
                x_ends[side, rows_cot, :] = other.astype(bf16)
        return carry

    lax.fori_loop(0, 16, plane, 0)
    x_ends[0, 512:528, :] = speeds[pl.ds(7, 16, stride=8), :].astype(bf16)
    x_ends[0, 528:544, :] = speeds[pl.ds(128 + 7, 16, stride=8), :].astype(bf16)
    x_ends[1, 512:544, :] = jnp.zeros((32, 128), bf16)
    pick = edge_picker(8, 1024)
    ends = mm(pick, s0[...], NT)
    ends_cot = mm(pick, v0[...].astype(bf16), NT)
    for side in (0, 1):
        y_ends[side, :, 0:256] = ends[side * 8 : side * 8 + 8]
        y_ends[side, :, 256:512] = ends_cot[side * 8 : side * 8 + 8]
    last = jnp.where(iota((8, 128), 1) == 127, 1.0, 0.0).astype(bf16)
    y_ends[0, :, 512:640] = mm(last, sy[...], NT)
    y_ends[0, :, 640:768] = mm(last, fy[...].astype(f32).astype(bf16), NT)
    y_ends[1, :, 512:768] = jnp.zeros((8, 256), f32)
    odd_x, odd_y = parities()
    x_even[...] = x_ends[odd_x]
    x_odd[...] = x_ends[1 - odd_x]
    y_even[0:8, :] = y_ends[odd_y]
    y_odd[0:8, :] = y_ends[1 - odd_y]


def parities():
    return lax.rem(lax.axis_index("y"), 2), lax.axis_index("c")


def forward_kernel(s0, weights, ones_all, twos_all, base):
    w_in, b_in, w_mid, b_mid, w_out, b_out = unbundled(weights)
    in_high, in_low = split(w_in[...])
    in_high, in_low = in_high.astype(f32), in_low.astype(f32)
    go_in = turned(jnp.concatenate([in_high, in_low, bias_rows(b_in[...])], 0))
    go_mid = turned(jnp.concatenate([stacked(w_mid[...]), bias_rows(b_mid[...])], 0))
    go_out = turned(jnp.concatenate([stacked((w_out[...] * 0.25).T), bias_rows(b_out[...] * 0.25)], 0))
    ones = jnp.full((16, PLANES * 1024), 1.0, bf16)

    def group(index, carry):
        rows = [pl.ds(pl.multiple_of((index * PLANES + i) * 16, 16), 16) for i in range(PLANES)]
        lanes = pl.ds(pl.multiple_of(index * PLANES * 1024, PLANES * 1024), PLANES * 1024)
        state = join([s0[r, :] for r in rows])
        one = jnp.tanh(mm(go_in, cat([state, state, ones])))
        ones_all[:, lanes] = one
        two = jnp.tanh(mm(go_mid, cat(three(split(one)) + [ones])))
        twos_all[:, lanes] = two
        result = state.astype(f32) + mm(go_out, cat(three(split(two)) + [ones]))
        for i, r in enumerate(rows):
            base[r, :] = result[:, i * 1024 : i * 1024 + 1024]
        return carry

    lax.fori_loop(0, 16 // PLANES, group, 0)


def unbundled(weights):
    return (
        weights.at[64:80, 0:64], weights.at[96:97, 0:64], weights.at[0:64, 0:64],
        weights.at[104:105, 0:64], weights.at[80:96, 0:64], weights.at[112:113, 0:16],
    )


def join(tiles):
    return jnp.concatenate(tiles, 1)


def cat(items):
    return jnp.concatenate(items, 0)


def stacked(matrix):
    high, low = split(matrix)
    high, low = high.astype(f32), low.astype(f32)
    return jnp.concatenate([high, high, low], 0)


def bias_rows(bias):
    first = bias.astype(bf16).astype(f32)
    rest = bias - first
    second = rest.astype(bf16).astype(f32)
    third = rest - second
    row = iota((16, bias.shape[1]), 0)
    return jnp.where(row == 0, first, jnp.where(row == 1, second, jnp.where(row == 2, third, 0.0)))


def turned(matrix):
    return matrix.T.astype(bf16)


def three(pair):
    return [pair[0], pair[1], pair[0]]


def main_kernel(
    ones_all, twos_all, base, s0, v0, speeds, x_odd, x_even, y_even, y_odd,
    weights,
    part, edge_coefs, x_even_out, x_odd_out, y_even_out, y_odd_out, sums,
    coefs, moment_ends, cot_ends, v1_held, total, x_got, y_got, x_ends, y_ends,
):
    w_in, b_in, w_mid, b_mid, w_out, _ = unbundled(weights)
    odd_x, odd_y = parities()
    x_got[1 - odd_x] = x_even[...]
    x_got[odd_x] = x_odd[...]
    y_got[1 - odd_y] = y_even[0:8, :]
    y_got[odd_y] = y_odd[0:8, :]
    x_prev, x_next, y_prev, y_next = x_got.at[0], x_got.at[1], y_got.at[0], y_got.at[1]
    flag = speeds[128:256, :] * 0.25
    speed = speeds[0:128, :]
    push_x, pull_x = speed * flag, speed * (0.25 - flag)
    flag = speeds[384:512, :] * 0.25
    speed = speeds[256:384, :]
    push_y, pull_y = speed * flag, speed * (0.25 - flag)
    row, lane = iota((128, 128), 0), iota((128, 128), 1)
    speed_prev = x_prev[512:528, :].astype(f32)
    flag_prev = x_prev[528:544, :].astype(f32) * 0.25
    wide = lambda item: jnp.broadcast_to(item[:, None, :], (16, 8, 128)).reshape(128, 128)
    first_row = lax.rem(row, 8) == 0
    pushed_x = jnp.where(first_row, wide(speed_prev * flag_prev), pltpu.roll(push_x, 1, 0))
    pulled_x = jnp.where(first_row, wide(speed_prev * (0.25 - flag_prev)), pltpu.roll(pull_x, 1, 0))
    place = jnp.where((iota((8, 128), 0) == 0) & (iota((8, 128), 1) == 0), 1.0, 0.0).astype(bf16)
    speed_prev = mm(y_prev[:, 512:640].astype(bf16), place, TN)
    flag_prev = mm(y_prev[:, 640:768].astype(bf16), place, TN) * 0.25
    pushed_y = jnp.where(lane == 0, speed_prev * flag_prev, pltpu.roll(push_y, 1, 1))
    pulled_y = jnp.where(lane == 0, speed_prev * (0.25 - flag_prev), pltpu.roll(pull_y, 1, 1))
    keep = push_x + pulled_x + push_y + pulled_y
    for index, item in enumerate(
        (keep, pull_x, pushed_x, pull_y, pushed_y, push_x, pulled_x, push_y, pulled_y)
    ):
        coefs[index * 128 : index * 128 + 128, :] = item
    for index, item in enumerate((push_x, pulled_x, push_y, pulled_y)):
        edge_coefs[index * 128 : index * 128 + 128, :] = item

    pick = edge_picker(8, 1024)
    ends = jnp.concatenate([y_next[:, 0:512], y_prev[:, 0:512]], 0).astype(bf16)
    moment_ends[...] = mm(ends[:, 0:256], pick, TN)
    cot_ends[...] = mm(ends[:, 256:512], pick, TN)

    w_in_, w_mid_ = w_in[...], w_mid[...]
    go_in = turned(jnp.concatenate([stacked(w_in_), bias_rows(b_in[...])], 0))
    go_mid = turned(jnp.concatenate([stacked(w_mid_), bias_rows(b_mid[...])], 0))
    back_out = turned(stacked(w_out[...] * 0.25))
    back_mid = turned(stacked(w_mid_.T))
    back_in = turned(stacked(w_in_.T))
    ones = jnp.full((16, PLANES * 1024), 1.0, bf16)
    zeros = jnp.zeros((16, PLANES * 1024), bf16)
    total[...] = jnp.zeros_like(total)
    end_lane = iota((16, 128), 1)

    def stencil(tiles, before, after, ends, z, first):
        around = [before] + tiles + [after]
        results = []
        for x in range(8):
            c = [
                coefs[pl.ds(k * 128 + z * 8 + x, 1), :] for k in (0, first, first + 1, first + 2, first + 3)
            ]
            here = around[x + 1]
            value = c[0] * here
            if around[x + 2] is not None:
                value = value - c[1] * around[x + 2]
            if around[x] is not None:
                value = value - c[2] * around[x]
            right, left = pltpu.roll(here, 127, 1), pltpu.roll(here, 1, 1)
            if ends is None:
                end = 0.0
            else:
                end = ends[x]
            right = jnp.where(end_lane == 127, end, right)
            left = jnp.where(end_lane == 0, end, left)
            value = value - c[3] * right - c[4] * left
            results.append(value)
        return results

    def tiles_of(value):
        return [value[:, x * 128 : x * 128 + 128] for x in range(8)]

    def layers(inputs):
        one = jnp.tanh(mm(go_in, cat(inputs)))
        one_pair = split(one)
        two = jnp.tanh(mm(go_mid, cat(three(one_pair) + [ones])))
        return one, one_pair, two, split(two)

    def backward(state_pair, one, one_pair, two, two_pair, adjoint):
        adjoint_pair = split(adjoint)
        grad_two = mm(back_out, cat(three(adjoint_pair))) * (1.0 - two * two)
        two_grad_pair = split(grad_two)
        grad_one = mm(back_mid, cat(three(two_grad_pair))) * (1.0 - one * one)
        one_grad_pair = split(grad_one)
        grad_cells = mm(back_in, cat(three(one_grad_pair)))
        left_high = cat([state_pair[0], one_pair[0], adjoint_pair[0], ones])
        left_low = cat([state_pair[1], one_pair[1], adjoint_pair[1], zeros])
        right_high = cat([two_grad_pair[0], one_grad_pair[0], two_pair[0], ones])
        right_low = cat([two_grad_pair[1], one_grad_pair[1], two_pair[1], zeros])
        both = mm(cat([left_high, left_low]), right_high, NT)
        total[:, 0:208] += both[0:112] + both[112:224] + mm(left_high, right_low, NT)
        return grad_cells

    def group(index, carry):
        planes = [index * PLANES + i for i in range(PLANES)]
        rows = [pl.ds(pl.multiple_of(z * 16, 16), 16) for z in planes]
        rows_cot = [pl.ds(pl.multiple_of(256 + z * 16, 16), 16) for z in planes]

        def moves(value, ends, edges, first):
            results = []
            for i, z in enumerate(planes):
                tiles = tiles_of(value[:, i * 1024 : i * 1024 + 1024])
                if ends is None:
                    results += stencil(tiles, None, None, None, z, first)
                else:
                    before, after = (ref[edges[i], :].astype(f32) for ref in (x_prev, x_next))
                    results += stencil(tiles, before, after, tiles_of(ends[rows[i], :]), z, first)
            return join(results)

        state_zero = join([s0[r, :] for r in rows])
        wide_state = state_zero.astype(f32)
        state_one = join([base[r, :] for r in rows]) - moves(wide_state, moment_ends, rows, 1)
        adjoint = join([v0[r, :] for r in rows])
        state_pair = split(state_one)
        saved = layers(three(state_pair) + [ones])
        grad_cells = backward(state_pair, *saved, adjoint)
        adjoint = adjoint + grad_cells - moves(adjoint, cot_ends, rows_cot, 5)
        for i, r in enumerate(rows):
            tile = adjoint[:, i * 1024 : i * 1024 + 1024]
            v1_held[r, :] = tile.astype(bf16)
            x_ends[0, r, :] = tile[:, 896:1024].astype(bf16)
            x_ends[1, r, :] = tile[:, 0:128].astype(bf16)
        lanes = pl.ds(pl.multiple_of(index * PLANES * 1024, PLANES * 1024), PLANES * 1024)
        one, two = ones_all[:, lanes], twos_all[:, lanes]
        grad_cells = backward((state_zero, zeros), one, split(one), two, split(two), adjoint)
        result = adjoint + grad_cells - moves(adjoint, None, None, 5)
        for i, r in enumerate(rows):
            part[r, :] = result[:, i * 1024 : i * 1024 + 1024]
        return carry

    lax.fori_loop(0, 16 // PLANES, group, 0)
    ends = mm(pick, v1_held[...], NT)
    y_ends[0] = ends[0:8]
    y_ends[1] = ends[8:16]
    x_even_out[...] = x_ends[odd_x]
    x_odd_out[...] = x_ends[1 - odd_x]
    y_even_out[...] = y_ends[odd_y]
    y_odd_out[...] = y_ends[1 - odd_y]
    first = total[:, 0:128]
    second = total[:, 128:256]
    turn = lambda item: pltpu.roll(item, 64, 1)
    rest = jnp.concatenate(
        [first[0:16], turn(second[80:96]), first[96:104], turn(first[96:104]), second[80:96]], 0
    )
    sums[...] = jnp.where(iota((64, 128), 1) < 64, first[16:80], rest)


def finish_kernel(part, edge_coefs, x_even, x_odd, y_even, y_odd, out, ends_held, x_got, y_got):
    odd_x, odd_y = parities()
    x_got[1 - odd_x] = x_even[...]
    x_got[odd_x] = x_odd[...]
    y_got[1 - odd_y] = y_even[...]
    y_got[odd_y] = y_odd[...]
    x_prev, x_next, y_prev, y_next = x_got.at[0], x_got.at[1], y_got.at[0], y_got.at[1]
    pick = edge_picker(8, 1024)
    ends = jnp.concatenate([y_next[...], y_prev[...]], 0).astype(bf16)
    ends_held[...] = mm(ends, pick, TN)
    end_lane = iota((1, 128), 1)

    def plane(z, carry):
        start = pl.multiple_of(z * 16, 16)
        rows = pl.ds(start, 16)
        for x in range(8):
            c = [edge_coefs[pl.ds(k * 128 + z * 8 + x, 1), :] for k in range(4)]
            value = part[rows, x * 128 : x * 128 + 128]
            weight = jnp.where(end_lane == 127, c[2], jnp.where(end_lane == 0, c[3], 0.0))
            value = value + weight * ends_held[rows, x * 128 : x * 128 + 128]
            if x == 7:
                value = value + c[0] * x_next[rows, :].astype(f32)
            if x == 0:
                value = value + c[1] * x_prev[rows, :].astype(f32)
            out[pl.ds(z * 8 + x, 16, stride=128), :] = value
        return carry

    lax.fori_loop(0, 16, plane, 0)


def weights_kernel(scale, mine, other, d_in, d_b_in, d_mid, d_b_mid, d_out, d_b_out):
    value = (mine[...] + other[...]) * scale
    moved = pltpu.roll(value, 64, 1)
    d_mid[...] = value[:, 0:64]
    d_in[...] = moved[0:16, 0:64]
    d_b_in[...] = moved[32:33, 0:64]
    d_b_mid[...] = moved[40:41, 0:64]
    d_out[...] = moved[16:32, 0:64] * 0.25
    d_b_out[...] = (moved[48:64, :] * 0.25).T[0:1, :]


def pairs(value, axis, links):
    return lax.ppermute(value, axis, [(a, b) for a, b in links] + [(b, a) for a, b in links])


def swapped(even, odd, axis, count):
    far = pairs(odd, axis, [(i, i + 1) for i in range(1, count - 1, 2)])
    return pairs(even, axis, [(i, i + 1) for i in range(0, count - 1, 2)]), far


def params(mebibytes):
    return pltpu.CompilerParams(vmem_limit_bytes=mebibytes * 1024 * 1024)


def cost(flops, size):
    return pl.CostEstimate(flops=flops, bytes_accessed=size, transcendentals=0)


def solution(mesh):
    parts = Mesh(mesh.devices.reshape(4, 4, 4, 2, 2), ("zh", "y", "x", "c", "zl"))
    gx, gy, sa = ("zh", "y"), ("x", "c"), "zl"
    ring = ("zh", "zl")
    wide = P(sa, None, None, gx, gy)
    flat = P(sa, None, gx, gy)
    cells = 4194304
    far = pl.BlockSpec(memory_space=pltpu.HBM)
    shape = jax.ShapeDtypeStruct

    def local(moments, speed_x, flag_x, speed_y, flag_y, w_in, b_in, w_mid, b_mid, w_out, b_out, final_cot):
        mom = moments.reshape(2048, 128)
        cot = final_cot.reshape(2048, 128)
        sx, fx, sy, fy = (item.reshape(128, 128) for item in (speed_x, flag_x, speed_y, flag_y))
        b_in, b_mid, b_out = b_in.reshape(1, 64), b_mid.reshape(1, 64), b_out.reshape(1, 16)
        w_out = w_out.T
        s0, v0, speeds, bundle, x_even, x_odd, y_even, y_odd = pl.pallas_call(
            pack_kernel,
            in_specs=[far] * 12,
            out_shape=(
                shape((256, 1024), bf16), shape((256, 1024), f32), shape((512, 128), f32),
                shape((128, 128), f32), shape((544, 128), bf16), shape((544, 128), bf16),
                shape((48, 768), f32), shape((48, 768), f32),
            ),
            scratch_shapes=[
                pltpu.VMEM((2048, 128), f32), pltpu.VMEM((2048, 128), bf16),
                pltpu.VMEM((128, 128), bf16), pltpu.VMEM((128, 128), jnp.int32),
                pltpu.VMEM((128, 128), bf16), pltpu.VMEM((128, 128), jnp.int32),
                pltpu.VMEM((16, 64), f32), pltpu.VMEM((1, 64), f32), pltpu.VMEM((64, 64), f32),
                pltpu.VMEM((1, 64), f32), pltpu.VMEM((16, 64), f32), pltpu.VMEM((1, 16), f32),
                pltpu.VMEM((2048, 128), f32), pltpu.VMEM((2, 544, 128), bf16),
                pltpu.VMEM((2, 8, 768), f32), pltpu.SemaphoreType.DMA((12,)),
            ],
            compiler_params=params(PACK),
            name="pack",
        )(cot, mom, sx, fx, sy, fy, w_in, b_in, w_mid, b_mid, w_out, b_out)
        x_even, x_odd = swapped(x_even, x_odd, gx, 16)
        y_even, y_odd = swapped(y_even, y_odd, gy, 8)
        ones_all, twos_all, base = pl.pallas_call(
            forward_kernel,
            out_shape=(shape((64, 16384), f32), shape((64, 16384), f32), shape((256, 1024), f32)),
            compiler_params=params(24),
            cost_estimate=cost(5000000000, 16000000),
            name="forward",
        )(s0, bundle)
        part, edge_coefs, x_even, x_odd, y_even, y_odd, sums = pl.pallas_call(
            main_kernel,
            out_shape=(
                shape((256, 1024), f32), shape((512, 128), f32),
                shape((256, 128), bf16), shape((256, 128), bf16),
                shape((8, 256), f32), shape((8, 256), f32), shape((64, 128), f32),
            ),
            scratch_shapes=[
                pltpu.VMEM((9 * 128, 128), f32), pltpu.VMEM((256, 1024), f32),
                pltpu.VMEM((256, 1024), f32), pltpu.VMEM((256, 1024), bf16),
                pltpu.VMEM((112, 256), f32), pltpu.VMEM((2, 544, 128), bf16),
                pltpu.VMEM((2, 8, 768), f32), pltpu.VMEM((2, 256, 128), bf16),
                pltpu.VMEM((2, 8, 256), f32),
            ],
            compiler_params=params(32),
            cost_estimate=cost(15000000000, 40000000),
            name="network",
        )(
            ones_all, twos_all, base, s0, v0, speeds, x_odd, x_even, y_even, y_odd, bundle
        )
        steps = (
            ("c", [(0, 1)]),
            ("x", [(0, 1), (2, 3)]),
            ("x", [(0, 3), (1, 2)]),
            ("y", [(0, 1), (2, 3)]),
            ("y", [(0, 3), (1, 2)]),
            (ring, [(0, 1), (2, 3), (4, 5), (6, 7)]),
            (ring, [(1, 2), (3, 4), (5, 6), (7, 0)]),
        )
        places = {
            "y_odd": (gy, y_odd, [(1, 2), (3, 4), (5, 6)]),
            "y_even": (gy, y_even, [(0, 1), (2, 3), (4, 5), (6, 7)]),
            "x_even": (gx, x_even, [(i, i + 1) for i in range(0, 15, 2)]),
            "x_odd": (gx, x_odd, [(i, i + 1) for i in range(1, 15, 2)]),
        }
        beside = {1: ("y_odd",), 2: ("y_even",), 3: ("x_even",), 4: ("x_odd",)}
        got = {}
        for index, (axis, links) in enumerate(steps):
            moving = {}
            for name in beside.get(index, ()):
                along, value, route = places[name]
                value, sums = lax.optimization_barrier((value, sums))
                moving[name] = pairs(value, along, route)
            sums = sums + pairs(sums, axis, links)
            if moving:
                names = list(moving)
                *values, sums = lax.optimization_barrier(tuple(moving[n] for n in names) + (sums,))
                got.update(zip(names, values))
        other = pairs(sums, ring, [(0, 3), (1, 6), (2, 5), (4, 7)])
        x_even, x_odd, y_even, y_odd = (got[n] for n in ("x_even", "x_odd", "y_even", "y_odd"))
        out = pl.pallas_call(
            finish_kernel,
            out_shape=shape((2048, 128), f32),
            scratch_shapes=[
                pltpu.VMEM((256, 1024), f32), pltpu.VMEM((2, 256, 128), bf16), pltpu.VMEM((2, 8, 256), f32)
            ],
            compiler_params=params(16),
            cost_estimate=cost(10000000, 6000000),
            name="finish",
        )(part, edge_coefs, x_even, x_odd, y_even, y_odd)

        d_in, d_b_in, d_mid, d_b_mid, d_out, d_b_out = pl.pallas_call(
            lambda *refs: weights_kernel(1.0 / cells, *refs),
            out_shape=(
                shape((16, 64), f32), shape((1, 64), f32), shape((64, 64), f32),
                shape((1, 64), f32), shape((16, 64), f32), shape((1, 16), f32),
            ),
            compiler_params=params(16),
            name="weights",
        )(sums, other)
        return (
            out.reshape(final_cot.shape), d_in, d_b_in.reshape(64), d_mid, d_b_mid.reshape(64),
            d_out.T, d_b_out.reshape(16),
        )

    return jax.shard_map(
        local,
        mesh=parts,
        in_specs=(wide, flat, flat, flat, flat, P(), P(), P(), P(), P(), P(), wide),
        out_specs=(wide, P(), P(), P(), P(), P(), P()),
        check_vma=False,
    )
```

```python
import jax
import jax.numpy as jnp
from jax import lax
from jax.experimental import pallas as pl
from jax.experimental.pallas import tpu as pltpu
from jax.sharding import Mesh, PartitionSpec as P

f32 = jnp.float32
bf16 = jnp.bfloat16

NN = (((1,), (0,)), ((), ()))
NT = (((1,), (1,)), ((), ()))
TN = (((0,), (0,)), ((), ()))
PLANES = 4
TAIL = 5
PACK = 56


def mm(a, b, dims=NN):
    return lax.dot_general(a, b, dims, preferred_element_type=f32)


def split(value):
    high = value.astype(bf16)
    return high, (value - high.astype(f32)).astype(bf16)


def iota(shape, dim):
    return lax.broadcasted_iota(jnp.int32, shape, dim)


def edge_picker(rows, length):
    row, lane = iota((2 * rows, length), 0), iota((2 * rows, length), 1)
    spot = jnp.where(row < rows, row * 128 + 127, (row - rows) * 128)
    return jnp.where(lane == spot, 1.0, 0.0).astype(bf16)


def pack_kernel(
    cot_far, mom_far, sx_far, fx_far, sy_far, fy_far,
    w_in_far, b_in_far, w_mid_far, b_mid_far, w_out_far, b_out_far,
    s0, v0, speeds, x_even, x_odd, y_even, y_odd,
    cot, mom, sx, fx, sy, fy, w_in, b_in, w_mid, b_mid, w_out, b_out,
    mom_wide, x_ends, y_ends, weights, sems,
):
    copies = [
        pltpu.make_async_copy(far, near, sems.at[i])
        for i, (far, near) in enumerate(
            (
                (cot_far, cot), (mom_far, mom), (sx_far, sx), (fx_far, fx), (sy_far, sy), (fy_far, fy),
                (w_in_far, w_in), (b_in_far, b_in), (w_mid_far, w_mid),
                (b_mid_far, b_mid), (w_out_far, w_out), (b_out_far, b_out),
            )
        )
    ]
    for copy in copies:
        copy.start()
    for copy in copies[1:]:
        copy.wait()
    mom_wide[...] = mom[...].astype(f32)
    for index, ref in enumerate((sx, fx, sy, fy)):
        speeds[index * 128 : index * 128 + 128, :] = ref[...].astype(f32)
    weights[...] = jnp.zeros((128, 128), f32)
    weights[0:64, 0:64] = w_mid[...]
    weights[64:80, 0:64] = w_in[...]
    weights[80:96, 0:64] = w_out[...]
    weights[96:97, 0:64] = b_in[...]
    weights[104:105, 0:64] = b_mid[...]
    weights[112:113, 0:16] = b_out[...]
    rest = weights[...]
    for term in range(3):
        piece = rest.astype(bf16)
        rest = rest - piece.astype(f32)
        for i in range(8):
            s0[256 + term * 16 : 272 + term * 16, i * 128 : i * 128 + 128] = piece[i * 16 : i * 16 + 16]
    copies[0].wait()

    def plane(z, carry):
        rows = pl.ds(pl.multiple_of(z * 16, 16), 16)
        rows_cot = pl.ds(pl.multiple_of(256 + z * 16, 16), 16)
        for x in range(8):
            tile = mom_wide[pl.ds(z * 8 + x, 16, stride=128), :].astype(bf16)
            other = cot[pl.ds(z * 8 + x, 16, stride=128), :]
            s0[rows, x * 128 : x * 128 + 128] = tile
            v0[rows, x * 128 : x * 128 + 128] = other
            if x in (0, 7):
                side = 0 if x == 7 else 1
                x_ends[side, rows, :] = tile
                x_ends[side, rows_cot, :] = other.astype(bf16)
        return carry

    lax.fori_loop(0, 16, plane, 0)
    x_ends[0, 512:528, :] = speeds[pl.ds(7, 16, stride=8), :].astype(bf16)
    x_ends[0, 528:544, :] = speeds[pl.ds(128 + 7, 16, stride=8), :].astype(bf16)
    x_ends[1, 512:544, :] = jnp.zeros((32, 128), bf16)
    pick = edge_picker(8, 1024)
    ends = mm(pick, s0[0:256, :], NT)
    ends_cot = mm(pick, v0[...].astype(bf16), NT)
    for side in (0, 1):
        y_ends[side, :, 0:256] = ends[side * 8 : side * 8 + 8]
        y_ends[side, :, 256:512] = ends_cot[side * 8 : side * 8 + 8]
    last = jnp.where(iota((8, 128), 1) == 127, 1.0, 0.0).astype(bf16)
    y_ends[0, :, 512:640] = mm(last, sy[...], NT)
    y_ends[0, :, 640:768] = mm(last, fy[...].astype(f32).astype(bf16), NT)
    y_ends[1, :, 512:768] = jnp.zeros((8, 256), f32)
    odd_x, odd_y = parities()
    x_even[...] = x_ends[odd_x]
    x_odd[...] = x_ends[1 - odd_x]
    y_even[0:8, :] = y_ends[odd_y]
    y_odd[0:8, :] = y_ends[1 - odd_y]


def parities():
    return lax.rem(lax.axis_index("y"), 2), lax.axis_index("c")


def forward_kernel(s0, ones_all, twos_all, base, weights):
    w_in, b_in, w_mid, b_mid, w_out, b_out = unbundled(s0, weights)
    in_high, in_low = split(w_in[...])
    in_high, in_low = in_high.astype(f32), in_low.astype(f32)
    go_in = turned(jnp.concatenate([in_high, in_low, bias_rows(b_in[...])], 0))
    go_mid = turned(jnp.concatenate([stacked(w_mid[...]), bias_rows(b_mid[...])], 0))
    go_out = turned(jnp.concatenate([stacked((w_out[...] * 0.25).T), bias_rows(b_out[...] * 0.25)], 0))
    ones = jnp.full((16, PLANES * 1024), 1.0, bf16)

    def group(index, carry):
        rows = [pl.ds(pl.multiple_of((index * PLANES + i) * 16, 16), 16) for i in range(PLANES)]
        lanes = pl.ds(pl.multiple_of(index * PLANES * 1024, PLANES * 1024), PLANES * 1024)
        state = join([s0[r, :] for r in rows])
        one = jnp.tanh(mm(go_in, cat([state, state, ones])))
        ones_all[:, lanes] = one
        two = jnp.tanh(mm(go_mid, cat(three(split(one)) + [ones])))
        twos_all[:, lanes] = two
        result = state.astype(f32) + mm(go_out, cat(three(split(two)) + [ones]))
        for i, r in enumerate(rows):
            base[r, :] = result[:, i * 1024 : i * 1024 + 1024]
        return carry

    lax.fori_loop(0, 16 // PLANES, group, 0)


def unbundled(cells, weights):
    for i in range(8):
        first, second, third = (
            cells[256 + term * 16 : 272 + term * 16, i * 128 : i * 128 + 128].astype(f32) for term in range(3)
        )
        weights[i * 16 : i * 16 + 16, :] = first + second + third
    return (
        weights.at[64:80, 0:64], weights.at[96:97, 0:64], weights.at[0:64, 0:64],
        weights.at[104:105, 0:64], weights.at[80:96, 0:64], weights.at[112:113, 0:16],
    )


def join(tiles):
    return jnp.concatenate(tiles, 1)


def cat(items):
    return jnp.concatenate(items, 0)


def stencil(coefs, tiles, before, after, ends, z, first):
    end_lane = iota((16, 128), 1)
    around = [before] + tiles + [after]
    results = []
    for x in range(8):
        c = [
            coefs[pl.ds(k * 128 + z * 8 + x, 1), :] for k in (0, first, first + 1, first + 2, first + 3)
        ]
        here = around[x + 1]
        value = c[0] * here
        if around[x + 2] is not None:
            value = value - c[1] * around[x + 2]
        if around[x] is not None:
            value = value - c[2] * around[x]
        right, left = pltpu.roll(here, 127, 1), pltpu.roll(here, 1, 1)
        if ends is None:
            end = 0.0
        else:
            end = ends[x]
        right = jnp.where(end_lane == 127, end, right)
        left = jnp.where(end_lane == 0, end, left)
        value = value - c[3] * right - c[4] * left
        results.append(value)
    return results


def tiles_of(value):
    return [value[:, x * 128 : x * 128 + 128] for x in range(8)]

def stacked(matrix):
    high, low = split(matrix)
    high, low = high.astype(f32), low.astype(f32)
    return jnp.concatenate([high, high, low], 0)


def bias_rows(bias):
    first = bias.astype(bf16).astype(f32)
    rest = bias - first
    second = rest.astype(bf16).astype(f32)
    third = rest - second
    row = iota((16, bias.shape[1]), 0)
    return jnp.where(row == 0, first, jnp.where(row == 1, second, jnp.where(row == 2, third, 0.0)))


def turned(matrix):
    return matrix.T.astype(bf16)


def three(pair):
    return [pair[0], pair[1], pair[0]]


def main_kernel(
    ones_all, twos_all, base, s0, v0, speeds, x_odd, x_even, y_even, y_odd,
    v1, coefs, ones_grad_high, ones_grad_low, x_even_out, x_odd_out, y_even_out, y_odd_out, sums,
    moment_ends, cot_ends, v1_held, total, x_got, y_got, x_ends, y_ends, weights,
):
    w_in, b_in, w_mid, b_mid, w_out, _ = unbundled(s0, weights)
    odd_x, odd_y = parities()
    x_got[1 - odd_x] = x_even[...]
    x_got[odd_x] = x_odd[...]
    y_got[1 - odd_y] = y_even[0:8, :]
    y_got[odd_y] = y_odd[0:8, :]
    x_prev, x_next, y_prev, y_next = x_got.at[0], x_got.at[1], y_got.at[0], y_got.at[1]
    flag = speeds[128:256, :] * 0.25
    speed = speeds[0:128, :]
    push_x, pull_x = speed * flag, speed * (0.25 - flag)
    flag = speeds[384:512, :] * 0.25
    speed = speeds[256:384, :]
    push_y, pull_y = speed * flag, speed * (0.25 - flag)
    row, lane = iota((128, 128), 0), iota((128, 128), 1)
    speed_prev = x_prev[512:528, :].astype(f32)
    flag_prev = x_prev[528:544, :].astype(f32) * 0.25
    wide = lambda item: jnp.broadcast_to(item[:, None, :], (16, 8, 128)).reshape(128, 128)
    first_row = lax.rem(row, 8) == 0
    pushed_x = jnp.where(first_row, wide(speed_prev * flag_prev), pltpu.roll(push_x, 1, 0))
    pulled_x = jnp.where(first_row, wide(speed_prev * (0.25 - flag_prev)), pltpu.roll(pull_x, 1, 0))
    place = jnp.where((iota((8, 128), 0) == 0) & (iota((8, 128), 1) == 0), 1.0, 0.0).astype(bf16)
    speed_prev = mm(y_prev[:, 512:640].astype(bf16), place, TN)
    flag_prev = mm(y_prev[:, 640:768].astype(bf16), place, TN) * 0.25
    pushed_y = jnp.where(lane == 0, speed_prev * flag_prev, pltpu.roll(push_y, 1, 1))
    pulled_y = jnp.where(lane == 0, speed_prev * (0.25 - flag_prev), pltpu.roll(pull_y, 1, 1))
    keep = push_x + pulled_x + push_y + pulled_y
    for index, item in enumerate(
        (keep, pull_x, pushed_x, pull_y, pushed_y, push_x, pulled_x, push_y, pulled_y)
    ):
        coefs[index * 128 : index * 128 + 128, :] = item

    pick = edge_picker(8, 1024)
    ends = jnp.concatenate([y_next[:, 0:512], y_prev[:, 0:512]], 0).astype(bf16)
    moment_ends[...] = mm(ends[:, 0:256], pick, TN)
    cot_ends[...] = mm(ends[:, 256:512], pick, TN)

    w_in_, w_mid_ = w_in[...], w_mid[...]
    go_in = turned(jnp.concatenate([stacked(w_in_), bias_rows(b_in[...])], 0))
    go_mid = turned(jnp.concatenate([stacked(w_mid_), bias_rows(b_mid[...])], 0))
    back_out = turned(stacked(w_out[...] * 0.25))
    back_mid = turned(stacked(w_mid_.T))
    back_in = turned(stacked(w_in_.T))
    ones = jnp.full((16, PLANES * 1024), 1.0, bf16)
    zeros = jnp.zeros((16, PLANES * 1024), bf16)
    total[...] = jnp.zeros_like(total)

    def layers(inputs):
        one = jnp.tanh(mm(go_in, cat(inputs)))
        one_pair = split(one)
        two = jnp.tanh(mm(go_mid, cat(three(one_pair) + [ones])))
        return one, one_pair, two, split(two)

    def backward(state_pair, one, one_pair, two, two_pair, adjoint):
        adjoint_pair = split(adjoint)
        grad_two = mm(back_out, cat(three(adjoint_pair))) * (1.0 - two * two)
        two_grad_pair = split(grad_two)
        grad_one = mm(back_mid, cat(three(two_grad_pair))) * (1.0 - one * one)
        one_grad_pair = split(grad_one)
        left_high = cat([state_pair[0], one_pair[0], adjoint_pair[0], ones])
        left_low = cat([state_pair[1], one_pair[1], adjoint_pair[1], zeros])
        right_high = cat([two_grad_pair[0], one_grad_pair[0], two_pair[0], ones])
        right_low = cat([two_grad_pair[1], one_grad_pair[1], two_pair[1], zeros])
        both = mm(cat([left_high, left_low]), right_high, NT)
        total[:, 0:208] += both[0:112] + both[112:224] + mm(left_high, right_low, NT)
        return one_grad_pair

    def group(index, carry):
        planes = [index * PLANES + i for i in range(PLANES)]
        rows = [pl.ds(pl.multiple_of(z * 16, 16), 16) for z in planes]
        rows_cot = [pl.ds(pl.multiple_of(256 + z * 16, 16), 16) for z in planes]

        def moves(value, ends, edges, first):
            results = []
            for i, z in enumerate(planes):
                tiles = tiles_of(value[:, i * 1024 : i * 1024 + 1024])
                before, after = (ref[edges[i], :].astype(f32) for ref in (x_prev, x_next))
                results += stencil(coefs, tiles, before, after, tiles_of(ends[rows[i], :]), z, first)
            return join(results)

        state_zero = join([s0[r, :] for r in rows])
        wide_state = state_zero.astype(f32)
        state_one = join([base[r, :] for r in rows]) - moves(wide_state, moment_ends, rows, 1)
        adjoint = join([v0[r, :] for r in rows])
        state_pair = split(state_one)
        saved = layers(three(state_pair) + [ones])
        grad_cells = mm(back_in, cat(three(backward(state_pair, *saved, adjoint))))
        adjoint = adjoint + grad_cells - moves(adjoint, cot_ends, rows_cot, 5)
        for i, r in enumerate(rows):
            tile = adjoint[:, i * 1024 : i * 1024 + 1024]
            v1_held[r, :] = tile.astype(bf16)
            v1[r, :] = tile
            x_ends[0, r, :] = tile[:, 896:1024].astype(bf16)
            x_ends[1, r, :] = tile[:, 0:128].astype(bf16)
        lanes = pl.ds(pl.multiple_of(index * PLANES * 1024, PLANES * 1024), PLANES * 1024)
        one, two = ones_all[:, lanes], twos_all[:, lanes]
        grad_pair = backward((state_zero, zeros), one, split(one), two, split(two), adjoint)
        ones_grad_high[:, lanes] = grad_pair[0]
        ones_grad_low[:, lanes] = grad_pair[1]
        return carry

    lax.fori_loop(0, 16 // PLANES, group, 0)
    ends = mm(pick, v1_held[...], NT)
    y_ends[0] = ends[0:8]
    y_ends[1] = ends[8:16]
    x_even_out[...] = x_ends[odd_x]
    x_odd_out[...] = x_ends[1 - odd_x]
    y_even_out[...] = y_ends[odd_y]
    y_odd_out[...] = y_ends[1 - odd_y]
    first = total[:, 0:128]
    second = total[:, 128:256]
    turn = lambda item: pltpu.roll(item, 64, 1)
    rest = jnp.concatenate(
        [first[0:16], turn(second[80:96]), first[96:104], turn(first[96:104]), second[80:96]], 0
    )
    sums[...] = jnp.where(iota((64, 128), 1) < 64, first[16:80], rest)


def tail_kernel(v1, coefs, grad_high, grad_low, s0, part, weights):
    back_in = turned(stacked(unbundled(s0, weights)[0][...].T))

    def group(index, carry):
        lanes = pl.ds(pl.multiple_of(index * PLANES * 1024, PLANES * 1024), PLANES * 1024)
        high, low = grad_high[:, lanes], grad_low[:, lanes]
        grad_cells = mm(back_in, cat([high, low, high]))
        for i in range(PLANES):
            z = index * PLANES + i
            rows = pl.ds(pl.multiple_of(z * 16, 16), 16)
            here = v1[rows, :]
            moved = stencil(coefs, tiles_of(here), None, None, None, z, 5)
            part[rows, :] = here + grad_cells[:, i * 1024 : i * 1024 + 1024] - join(moved)
        return carry

    lax.fori_loop(0, 16 // PLANES, group, 0)


def finish_kernel(part, coefs, x_even, x_odd, y_even, y_odd, out, ends_held, x_got, y_got):
    odd_x, odd_y = parities()
    x_got[1 - odd_x] = x_even[...]
    x_got[odd_x] = x_odd[...]
    y_got[1 - odd_y] = y_even[...]
    y_got[odd_y] = y_odd[...]
    x_prev, x_next, y_prev, y_next = x_got.at[0], x_got.at[1], y_got.at[0], y_got.at[1]
    pick = edge_picker(8, 1024)
    ends = jnp.concatenate([y_next[...], y_prev[...]], 0).astype(bf16)
    ends_held[...] = mm(ends, pick, TN)
    end_lane = iota((1, 128), 1)

    def plane(z, carry):
        start = pl.multiple_of(z * 16, 16)
        rows = pl.ds(start, 16)
        for x in range(8):
            c = [coefs[pl.ds(k * 128 + z * 8 + x, 1), :] for k in (5, 6, 7, 8)]
            value = part[rows, x * 128 : x * 128 + 128]
            weight = jnp.where(end_lane == 127, c[2], jnp.where(end_lane == 0, c[3], 0.0))
            value = value + weight * ends_held[rows, x * 128 : x * 128 + 128]
            if x == 7:
                value = value + c[0] * x_next[rows, :].astype(f32)
            if x == 0:
                value = value + c[1] * x_prev[rows, :].astype(f32)
            out[pl.ds(z * 8 + x, 16, stride=128), :] = value
        return carry

    lax.fori_loop(0, 16, plane, 0)


def weights_kernel(scale, mine, other, d_in, d_b_in, d_mid, d_b_mid, d_out, d_b_out):
    value = (mine[...] + other[...]) * scale
    moved = pltpu.roll(value, 64, 1)
    d_mid[...] = value[:, 0:64]
    d_in[...] = moved[0:16, 0:64]
    d_b_in[...] = moved[32:33, 0:64]
    d_b_mid[...] = moved[40:41, 0:64]
    d_out[...] = moved[16:32, 0:64] * 0.25
    d_b_out[...] = (moved[48:64, :] * 0.25).T[0:1, :]


def pairs(value, axis, links):
    return lax.ppermute(value, axis, [(a, b) for a, b in links] + [(b, a) for a, b in links])


def swapped(even, odd, axis, count):
    far = pairs(odd, axis, [(i, i + 1) for i in range(1, count - 1, 2)])
    return pairs(even, axis, [(i, i + 1) for i in range(0, count - 1, 2)]), far


def params(mebibytes):
    return pltpu.CompilerParams(vmem_limit_bytes=mebibytes * 1024 * 1024)


def cost(flops, size):
    return pl.CostEstimate(flops=flops, bytes_accessed=size, transcendentals=0)


def solution(mesh):
    parts = Mesh(mesh.devices.reshape(4, 4, 4, 2, 2), ("zh", "y", "x", "c", "zl"))
    gx, gy, sa = ("zh", "y"), ("x", "c"), "zl"
    ring = ("zh", "zl")
    wide = P(sa, None, None, gx, gy)
    flat = P(sa, None, gx, gy)
    cells = 4194304
    far = pl.BlockSpec(memory_space=pltpu.HBM)
    shape = jax.ShapeDtypeStruct

    def local(moments, speed_x, flag_x, speed_y, flag_y, w_in, b_in, w_mid, b_mid, w_out, b_out, final_cot):
        mom = moments.reshape(2048, 128)
        cot = final_cot.reshape(2048, 128)
        sx, fx, sy, fy = (item.reshape(128, 128) for item in (speed_x, flag_x, speed_y, flag_y))
        b_in, b_mid, b_out = b_in.reshape(1, 64), b_mid.reshape(1, 64), b_out.reshape(1, 16)
        w_out = w_out.T
        s0, v0, speeds, x_even, x_odd, y_even, y_odd = pl.pallas_call(
            pack_kernel,
            in_specs=[far] * 12,
            out_shape=(
                shape((304, 1024), bf16), shape((256, 1024), f32), shape((512, 128), f32),
                shape((544, 128), bf16), shape((544, 128), bf16),
                shape((48, 768), f32), shape((48, 768), f32),
            ),
            scratch_shapes=[
                pltpu.VMEM((2048, 128), f32), pltpu.VMEM((2048, 128), bf16),
                pltpu.VMEM((128, 128), bf16), pltpu.VMEM((128, 128), jnp.int32),
                pltpu.VMEM((128, 128), bf16), pltpu.VMEM((128, 128), jnp.int32),
                pltpu.VMEM((16, 64), f32), pltpu.VMEM((1, 64), f32), pltpu.VMEM((64, 64), f32),
                pltpu.VMEM((1, 64), f32), pltpu.VMEM((16, 64), f32), pltpu.VMEM((1, 16), f32),
                pltpu.VMEM((2048, 128), f32), pltpu.VMEM((2, 544, 128), bf16),
                pltpu.VMEM((2, 8, 768), f32), pltpu.VMEM((128, 128), f32), pltpu.SemaphoreType.DMA((12,)),
            ],
            compiler_params=params(PACK),
            name="pack",
        )(cot, mom, sx, fx, sy, fy, w_in, b_in, w_mid, b_mid, w_out, b_out)
        x_even, x_odd = swapped(x_even, x_odd, gx, 16)
        y_even, y_odd = swapped(y_even, y_odd, gy, 8)
        ones_all, twos_all, base = pl.pallas_call(
            forward_kernel,
            out_shape=(shape((64, 16384), f32), shape((64, 16384), f32), shape((256, 1024), f32)),
            scratch_shapes=[pltpu.VMEM((128, 128), f32)],
            compiler_params=params(24),
            cost_estimate=cost(5000000000, 16000000),
            name="forward",
        )(s0)
        v1, coefs, grad_high, grad_low, x_even, x_odd, y_even, y_odd, sums = pl.pallas_call(
            main_kernel,
            out_shape=(
                shape((256, 1024), f32), shape((9 * 128, 128), f32),
                shape((64, 16384), bf16), shape((64, 16384), bf16),
                shape((256, 128), bf16), shape((256, 128), bf16),
                shape((8, 256), f32), shape((8, 256), f32), shape((64, 128), f32),
            ),
            scratch_shapes=[
                pltpu.VMEM((256, 1024), f32),
                pltpu.VMEM((256, 1024), f32), pltpu.VMEM((256, 1024), bf16),
                pltpu.VMEM((112, 256), f32), pltpu.VMEM((2, 544, 128), bf16),
                pltpu.VMEM((2, 8, 768), f32), pltpu.VMEM((2, 256, 128), bf16),
                pltpu.VMEM((2, 8, 256), f32), pltpu.VMEM((128, 128), f32),
            ],
            compiler_params=params(32),
            cost_estimate=cost(15000000000, 40000000),
            name="network",
        )(
            ones_all, twos_all, base, s0, v0, speeds, x_odd, x_even, y_even, y_odd
        )
        steps = (
            ("c", [(0, 1)]),
            ("x", [(0, 1), (2, 3)]),
            ("x", [(0, 3), (1, 2)]),
            ("y", [(0, 1), (2, 3)]),
            ("y", [(0, 3), (1, 2)]),
            (ring, [(0, 1), (2, 3), (4, 5), (6, 7)]),
            (ring, [(1, 2), (3, 4), (5, 6), (7, 0)]),
        )
        places = {
            "y_odd": (gy, y_odd, [(1, 2), (3, 4), (5, 6)]),
            "y_even": (gy, y_even, [(0, 1), (2, 3), (4, 5), (6, 7)]),
            "x_even": (gx, x_even, [(i, i + 1) for i in range(0, 15, 2)]),
            "x_odd": (gx, x_odd, [(i, i + 1) for i in range(1, 15, 2)]),
        }
        beside = {1: ("y_odd",), 2: ("y_even",), 3: ("x_even",), 4: ("x_odd",)}
        got = {}
        for index, (axis, links) in enumerate(steps):
            moving = {}
            for name in beside.get(index, ()):
                along, value, route = places[name]
                value, sums = lax.optimization_barrier((value, sums))
                moving[name] = pairs(value, along, route)
            if index == TAIL:
                v1, sums = lax.optimization_barrier((v1, sums))
                part = pl.pallas_call(
                    tail_kernel,
                    out_shape=shape((256, 1024), f32),
                    scratch_shapes=[pltpu.VMEM((128, 128), f32)],
                    compiler_params=params(16),
                    cost_estimate=cost(2000000000, 8000000),
                    name="tail",
                )(v1, coefs, grad_high, grad_low, s0)
            sums = sums + pairs(sums, axis, links)
            if index == TAIL:
                part, sums = lax.optimization_barrier((part, sums))
            if moving:
                names = list(moving)
                *values, sums = lax.optimization_barrier(tuple(moving[n] for n in names) + (sums,))
                got.update(zip(names, values))
        other = pairs(sums, ring, [(0, 3), (1, 6), (2, 5), (4, 7)])
        x_even, x_odd, y_even, y_odd = (got[n] for n in ("x_even", "x_odd", "y_even", "y_odd"))
        out = pl.pallas_call(
            finish_kernel,
            out_shape=shape((2048, 128), f32),
            scratch_shapes=[
                pltpu.VMEM((256, 1024), f32), pltpu.VMEM((2, 256, 128), bf16), pltpu.VMEM((2, 8, 256), f32)
            ],
            compiler_params=params(16),
            cost_estimate=cost(10000000, 6000000),
            name="finish",
        )(part, coefs, x_even, x_odd, y_even, y_odd)

        d_in, d_b_in, d_mid, d_b_mid, d_out, d_b_out = pl.pallas_call(
            lambda *refs: weights_kernel(1.0 / cells, *refs),
            out_shape=(
                shape((16, 64), f32), shape((1, 64), f32), shape((64, 64), f32),
                shape((1, 64), f32), shape((16, 64), f32), shape((1, 16), f32),
            ),
            compiler_params=params(16),
            name="weights",
        )(sums, other)
        return (
            out.reshape(final_cot.shape), d_in, d_b_in.reshape(64), d_mid, d_b_mid.reshape(64),
            d_out.T, d_b_out.reshape(16),
        )

    return jax.shard_map(
        local,
        mesh=parts,
        in_specs=(wide, flat, flat, flat, flat, P(), P(), P(), P(), P(), P(), wide),
        out_specs=(wide, P(), P(), P(), P(), P(), P()),
        check_vma=False,
    )
```

```python
import jax
import jax.numpy as jnp
from jax import lax
from jax.experimental import pallas as pl
from jax.experimental.pallas import tpu as pltpu
from jax.sharding import Mesh, PartitionSpec as P

f32 = jnp.float32
bf16 = jnp.bfloat16

NN = (((1,), (0,)), ((), ()))
NT = (((1,), (1,)), ((), ()))
TN = (((0,), (0,)), ((), ()))
PLANES = 4
TAIL = 3
PACK = 56


def mm(a, b, dims=NN):
    return lax.dot_general(a, b, dims, preferred_element_type=f32)


def split(value):
    high = value.astype(bf16)
    return high, (value - high.astype(f32)).astype(bf16)


def iota(shape, dim):
    return lax.broadcasted_iota(jnp.int32, shape, dim)


def edge_picker(rows, length):
    row, lane = iota((2 * rows, length), 0), iota((2 * rows, length), 1)
    spot = jnp.where(row < rows, row * 128 + 127, (row - rows) * 128)
    return jnp.where(lane == spot, 1.0, 0.0).astype(bf16)


def pack_kernel(
    cot_far, mom_far, sx_far, fx_far, sy_far, fy_far,
    w_in_far, b_in_far, w_mid_far, b_mid_far, w_out_far, b_out_far,
    s0, v0, speeds, x_even, x_odd, y_even, y_odd,
    cot, mom, sx, fx, sy, fy, w_in, b_in, w_mid, b_mid, w_out, b_out,
    mom_wide, x_ends, y_ends, weights, sems,
):
    copies = [
        pltpu.make_async_copy(far, near, sems.at[i])
        for i, (far, near) in enumerate(
            (
                (cot_far, cot), (mom_far, mom), (sx_far, sx), (fx_far, fx), (sy_far, sy), (fy_far, fy),
                (w_in_far, w_in), (b_in_far, b_in), (w_mid_far, w_mid),
                (b_mid_far, b_mid), (w_out_far, w_out), (b_out_far, b_out),
            )
        )
    ]
    for copy in copies:
        copy.start()
    for copy in copies[1:]:
        copy.wait()
    mom_wide[...] = mom[...].astype(f32)
    for index, ref in enumerate((sx, fx, sy, fy)):
        speeds[index * 128 : index * 128 + 128, :] = ref[...].astype(f32)
    weights[...] = jnp.zeros((128, 128), f32)
    weights[0:64, 0:64] = w_mid[...]
    weights[64:80, 0:64] = w_in[...]
    weights[80:96, 0:64] = w_out[...]
    weights[96:97, 0:64] = b_in[...]
    weights[104:105, 0:64] = b_mid[...]
    weights[112:113, 0:16] = b_out[...]
    rest = weights[...]
    for term in range(3):
        piece = rest.astype(bf16)
        rest = rest - piece.astype(f32)
        for i in range(8):
            s0[256 + term * 16 : 272 + term * 16, i * 128 : i * 128 + 128] = piece[i * 16 : i * 16 + 16]
    copies[0].wait()

    def plane(z, carry):
        rows = pl.ds(pl.multiple_of(z * 16, 16), 16)
        rows_cot = pl.ds(pl.multiple_of(256 + z * 16, 16), 16)
        for x in range(8):
            tile = mom_wide[pl.ds(z * 8 + x, 16, stride=128), :].astype(bf16)
            other = cot[pl.ds(z * 8 + x, 16, stride=128), :]
            s0[rows, x * 128 : x * 128 + 128] = tile
            v0[rows, x * 128 : x * 128 + 128] = other
            if x in (0, 7):
                side = 0 if x == 7 else 1
                x_ends[side, rows, :] = tile
                x_ends[side, rows_cot, :] = other.astype(bf16)
        return carry

    lax.fori_loop(0, 16, plane, 0)
    x_ends[0, 512:528, :] = speeds[pl.ds(7, 16, stride=8), :].astype(bf16)
    x_ends[0, 528:544, :] = speeds[pl.ds(128 + 7, 16, stride=8), :].astype(bf16)
    x_ends[1, 512:544, :] = jnp.zeros((32, 128), bf16)
    pick = edge_picker(8, 1024)
    ends = mm(pick, s0[0:256, :], NT)
    ends_cot = mm(pick, v0[...].astype(bf16), NT)
    for side in (0, 1):
        y_ends[side, :, 0:256] = ends[side * 8 : side * 8 + 8]
        y_ends[side, :, 256:512] = ends_cot[side * 8 : side * 8 + 8]
    last = jnp.where(iota((8, 128), 1) == 127, 1.0, 0.0).astype(bf16)
    y_ends[0, :, 512:640] = mm(last, sy[...], NT)
    y_ends[0, :, 640:768] = mm(last, fy[...].astype(f32).astype(bf16), NT)
    y_ends[1, :, 512:768] = jnp.zeros((8, 256), f32)
    odd_x, odd_y = parities()
    x_even[...] = x_ends[odd_x]
    x_odd[...] = x_ends[1 - odd_x]
    y_even[0:8, :] = y_ends[odd_y]
    y_odd[0:8, :] = y_ends[1 - odd_y]


def parities():
    return lax.rem(lax.axis_index("y"), 2), lax.axis_index("c")


def forward_kernel(s0, ones_all, twos_all, base, weights):
    w_in, b_in, w_mid, b_mid, w_out, b_out = unbundled(s0, weights)
    in_high, in_low = split(w_in[...])
    in_high, in_low = in_high.astype(f32), in_low.astype(f32)
    go_in = turned(jnp.concatenate([in_high, in_low, bias_rows(b_in[...])], 0))
    go_mid = turned(jnp.concatenate([stacked(w_mid[...]), bias_rows(b_mid[...])], 0))
    go_out = turned(jnp.concatenate([stacked((w_out[...] * 0.25).T), bias_rows(b_out[...] * 0.25)], 0))
    ones = jnp.full((16, PLANES * 1024), 1.0, bf16)

    def group(index, carry):
        rows = [pl.ds(pl.multiple_of((index * PLANES + i) * 16, 16), 16) for i in range(PLANES)]
        lanes = pl.ds(pl.multiple_of(index * PLANES * 1024, PLANES * 1024), PLANES * 1024)
        state = join([s0[r, :] for r in rows])
        one = jnp.tanh(mm(go_in, cat([state, state, ones])))
        ones_all[:, lanes] = one
        two = jnp.tanh(mm(go_mid, cat(three(split(one)) + [ones])))
        twos_all[:, lanes] = two
        result = state.astype(f32) + mm(go_out, cat(three(split(two)) + [ones]))
        for i, r in enumerate(rows):
            base[r, :] = result[:, i * 1024 : i * 1024 + 1024]
        return carry

    lax.fori_loop(0, 16 // PLANES, group, 0)


def unbundled(cells, weights):
    for i in range(8):
        first, second, third = (
            cells[256 + term * 16 : 272 + term * 16, i * 128 : i * 128 + 128].astype(f32) for term in range(3)
        )
        weights[i * 16 : i * 16 + 16, :] = first + second + third
    return (
        weights.at[64:80, 0:64], weights.at[96:97, 0:64], weights.at[0:64, 0:64],
        weights.at[104:105, 0:64], weights.at[80:96, 0:64], weights.at[112:113, 0:16],
    )


def join(tiles):
    return jnp.concatenate(tiles, 1)


def cat(items):
    return jnp.concatenate(items, 0)


def stencil(coefs, tiles, before, after, ends, z, first):
    end_lane = iota((16, 128), 1)
    around = [before] + tiles + [after]
    results = []
    for x in range(8):
        c = [
            coefs[pl.ds(k * 128 + z * 8 + x, 1), :] for k in (0, first, first + 1, first + 2, first + 3)
        ]
        here = around[x + 1]
        value = c[0] * here
        if around[x + 2] is not None:
            value = value - c[1] * around[x + 2]
        if around[x] is not None:
            value = value - c[2] * around[x]
        right, left = pltpu.roll(here, 127, 1), pltpu.roll(here, 1, 1)
        if ends is None:
            end = 0.0
        else:
            end = ends[x]
        right = jnp.where(end_lane == 127, end, right)
        left = jnp.where(end_lane == 0, end, left)
        value = value - c[3] * right - c[4] * left
        results.append(value)
    return results


def tiles_of(value):
    return [value[:, x * 128 : x * 128 + 128] for x in range(8)]

def stacked(matrix):
    high, low = split(matrix)
    high, low = high.astype(f32), low.astype(f32)
    return jnp.concatenate([high, high, low], 0)


def bias_rows(bias):
    first = bias.astype(bf16).astype(f32)
    rest = bias - first
    second = rest.astype(bf16).astype(f32)
    third = rest - second
    row = iota((16, bias.shape[1]), 0)
    return jnp.where(row == 0, first, jnp.where(row == 1, second, jnp.where(row == 2, third, 0.0)))


def turned(matrix):
    return matrix.T.astype(bf16)


def three(pair):
    return [pair[0], pair[1], pair[0]]


def main_kernel(
    ones_all, twos_all, base, s0, v0, speeds, x_odd, x_even, y_even, y_odd,
    v1, coefs, ones_grad_high, ones_grad_low, x_even_out, x_odd_out, y_odd_out, sums,
    moment_ends, cot_ends, v1_held, total, x_got, y_got, x_ends, y_ends, weights,
):
    w_in, b_in, w_mid, b_mid, w_out, _ = unbundled(s0, weights)
    odd_x, odd_y = parities()
    x_got[1 - odd_x] = x_even[...]
    x_got[odd_x] = x_odd[...]
    y_got[1 - odd_y] = y_even[0:8, :]
    y_got[odd_y] = y_odd[0:8, :]
    x_prev, x_next, y_prev, y_next = x_got.at[0], x_got.at[1], y_got.at[0], y_got.at[1]
    flag = speeds[128:256, :] * 0.25
    speed = speeds[0:128, :]
    push_x, pull_x = speed * flag, speed * (0.25 - flag)
    flag = speeds[384:512, :] * 0.25
    speed = speeds[256:384, :]
    push_y, pull_y = speed * flag, speed * (0.25 - flag)
    row, lane = iota((128, 128), 0), iota((128, 128), 1)
    speed_prev = x_prev[512:528, :].astype(f32)
    flag_prev = x_prev[528:544, :].astype(f32) * 0.25
    wide = lambda item: jnp.broadcast_to(item[:, None, :], (16, 8, 128)).reshape(128, 128)
    first_row = lax.rem(row, 8) == 0
    pushed_x = jnp.where(first_row, wide(speed_prev * flag_prev), pltpu.roll(push_x, 1, 0))
    pulled_x = jnp.where(first_row, wide(speed_prev * (0.25 - flag_prev)), pltpu.roll(pull_x, 1, 0))
    place = jnp.where((iota((8, 128), 0) == 0) & (iota((8, 128), 1) == 0), 1.0, 0.0).astype(bf16)
    speed_prev = mm(y_prev[:, 512:640].astype(bf16), place, TN)
    flag_prev = mm(y_prev[:, 640:768].astype(bf16), place, TN) * 0.25
    pushed_y = jnp.where(lane == 0, speed_prev * flag_prev, pltpu.roll(push_y, 1, 1))
    pulled_y = jnp.where(lane == 0, speed_prev * (0.25 - flag_prev), pltpu.roll(pull_y, 1, 1))
    keep = push_x + pulled_x + push_y + pulled_y
    for index, item in enumerate(
        (keep, pull_x, pushed_x, pull_y, pushed_y, push_x, pulled_x, push_y, pulled_y)
    ):
        coefs[index * 128 : index * 128 + 128, :] = item

    pick = edge_picker(8, 1024)
    ends = jnp.concatenate([y_next[:, 0:512], y_prev[:, 0:512]], 0).astype(bf16)
    moment_ends[...] = mm(ends[:, 0:256], pick, TN)
    cot_ends[...] = mm(ends[:, 256:512], pick, TN)

    w_in_, w_mid_ = w_in[...], w_mid[...]
    go_in = turned(jnp.concatenate([stacked(w_in_), bias_rows(b_in[...])], 0))
    go_mid = turned(jnp.concatenate([stacked(w_mid_), bias_rows(b_mid[...])], 0))
    back_out = turned(stacked(w_out[...] * 0.25))
    back_mid = turned(stacked(w_mid_.T))
    back_in = turned(stacked(w_in_.T))
    ones = jnp.full((16, PLANES * 1024), 1.0, bf16)
    zeros = jnp.zeros((16, PLANES * 1024), bf16)
    total[...] = jnp.zeros_like(total)

    def layers(inputs):
        one = jnp.tanh(mm(go_in, cat(inputs)))
        one_pair = split(one)
        two = jnp.tanh(mm(go_mid, cat(three(one_pair) + [ones])))
        return one, one_pair, two, split(two)

    def backward(state_pair, one, one_pair, two, two_pair, adjoint):
        adjoint_pair = split(adjoint)
        grad_two = mm(back_out, cat(three(adjoint_pair))) * (1.0 - two * two)
        two_grad_pair = split(grad_two)
        grad_one = mm(back_mid, cat(three(two_grad_pair))) * (1.0 - one * one)
        one_grad_pair = split(grad_one)
        left_high = cat([state_pair[0], one_pair[0], adjoint_pair[0], ones])
        left_low = cat([state_pair[1], one_pair[1], adjoint_pair[1], zeros])
        right_high = cat([two_grad_pair[0], one_grad_pair[0], two_pair[0], ones])
        right_low = cat([two_grad_pair[1], one_grad_pair[1], two_pair[1], zeros])
        both = mm(cat([left_high, left_low]), right_high, NT)
        total[:, 0:208] += both[0:112] + both[112:224] + mm(left_high, right_low, NT)
        return one_grad_pair

    def group(index, carry):
        planes = [index * PLANES + i for i in range(PLANES)]
        rows = [pl.ds(pl.multiple_of(z * 16, 16), 16) for z in planes]
        rows_cot = [pl.ds(pl.multiple_of(256 + z * 16, 16), 16) for z in planes]

        def moves(value, ends, edges, first):
            results = []
            for i, z in enumerate(planes):
                tiles = tiles_of(value[:, i * 1024 : i * 1024 + 1024])
                before, after = (ref[edges[i], :].astype(f32) for ref in (x_prev, x_next))
                results += stencil(coefs, tiles, before, after, tiles_of(ends[rows[i], :]), z, first)
            return join(results)

        state_zero = join([s0[r, :] for r in rows])
        wide_state = state_zero.astype(f32)
        state_one = join([base[r, :] for r in rows]) - moves(wide_state, moment_ends, rows, 1)
        adjoint = join([v0[r, :] for r in rows])
        state_pair = split(state_one)
        saved = layers(three(state_pair) + [ones])
        grad_cells = mm(back_in, cat(three(backward(state_pair, *saved, adjoint))))
        adjoint = adjoint + grad_cells - moves(adjoint, cot_ends, rows_cot, 5)
        for i, r in enumerate(rows):
            tile = adjoint[:, i * 1024 : i * 1024 + 1024]
            v1_held[r, :] = tile.astype(bf16)
            v1[r, :] = tile
            x_ends[0, r, :] = tile[:, 896:1024].astype(bf16)
            x_ends[1, r, :] = tile[:, 0:128].astype(bf16)
        lanes = pl.ds(pl.multiple_of(index * PLANES * 1024, PLANES * 1024), PLANES * 1024)
        one, two = ones_all[:, lanes], twos_all[:, lanes]
        grad_pair = backward((state_zero, zeros), one, split(one), two, split(two), adjoint)
        ones_grad_high[:, lanes] = grad_pair[0]
        ones_grad_low[:, lanes] = grad_pair[1]
        return carry

    lax.fori_loop(0, 16 // PLANES, group, 0)
    ends = mm(pick, v1_held[...], NT)
    y_ends[0] = ends[0:8]
    y_ends[1] = ends[8:16]
    x_even_out[...] = x_ends[odd_x]
    x_odd_out[...] = x_ends[1 - odd_x]
    ends = y_ends[1 - odd_y]
    y_odd_out[0:8, :] = ends[:, 0:128]
    y_odd_out[8:16, :] = ends[:, 128:256]
    ends = y_ends[odd_y]
    sums[64:72, :] = ends[:, 0:128]
    sums[72:80, :] = ends[:, 128:256]
    first = total[:, 0:128]
    second = total[:, 128:256]
    turn = lambda item: pltpu.roll(item, 64, 1)
    rest = jnp.concatenate(
        [first[0:16], turn(second[80:96]), first[96:104], turn(first[96:104]), second[80:96]], 0
    )
    sums[0:64, :] = jnp.where(iota((64, 128), 1) < 64, first[16:80], rest)


def tail_kernel(v1, coefs, grad_high, grad_low, s0, part, weights):
    back_in = turned(stacked(unbundled(s0, weights)[0][...].T))

    def group(index, carry):
        lanes = pl.ds(pl.multiple_of(index * PLANES * 1024, PLANES * 1024), PLANES * 1024)
        high, low = grad_high[:, lanes], grad_low[:, lanes]
        grad_cells = mm(back_in, cat([high, low, high]))
        for i in range(PLANES):
            z = index * PLANES + i
            rows = pl.ds(pl.multiple_of(z * 16, 16), 16)
            here = v1[rows, :]
            moved = stencil(coefs, tiles_of(here), None, None, None, z, 5)
            part[rows, :] = here + grad_cells[:, i * 1024 : i * 1024 + 1024] - join(moved)
        return carry

    lax.fori_loop(0, 16 // PLANES, group, 0)


def finish_kernel(part, coefs, x_even, x_odd, y_even, y_odd, out, ends_held, x_got, y_got):
    odd_x, odd_y = parities()
    x_got[1 - odd_x] = x_even[...]
    x_got[odd_x] = x_odd[...]
    at_end = jnp.logical_and(lax.axis_index("x") == 3, odd_y == 1)
    for half in (0, 1):
        rows, lanes = slice(64 + half * 8, 72 + half * 8), slice(half * 128, half * 128 + 128)
        y_got[1 - odd_y, :, lanes] = y_even[rows, :]
        y_got[odd_y, :, lanes] = jnp.where(at_end, 0.0, y_odd[rows, :])
    x_prev, x_next, y_prev, y_next = x_got.at[0], x_got.at[1], y_got.at[0], y_got.at[1]
    pick = edge_picker(8, 1024)
    ends = jnp.concatenate([y_next[...], y_prev[...]], 0).astype(bf16)
    ends_held[...] = mm(ends, pick, TN)
    end_lane = iota((1, 128), 1)

    def plane(z, carry):
        start = pl.multiple_of(z * 16, 16)
        rows = pl.ds(start, 16)
        for x in range(8):
            c = [coefs[pl.ds(k * 128 + z * 8 + x, 1), :] for k in (5, 6, 7, 8)]
            value = part[rows, x * 128 : x * 128 + 128]
            weight = jnp.where(end_lane == 127, c[2], jnp.where(end_lane == 0, c[3], 0.0))
            value = value + weight * ends_held[rows, x * 128 : x * 128 + 128]
            if x == 7:
                value = value + c[0] * x_next[rows, :].astype(f32)
            if x == 0:
                value = value + c[1] * x_prev[rows, :].astype(f32)
            out[pl.ds(z * 8 + x, 16, stride=128), :] = value
        return carry

    lax.fori_loop(0, 16, plane, 0)


def weights_kernel(scale, mine, other, d_in, d_b_in, d_mid, d_b_mid, d_out, d_b_out):
    value = (mine[...] + other[...]) * scale
    moved = pltpu.roll(value, 64, 1)
    d_mid[...] = value[:, 0:64]
    d_in[...] = moved[0:16, 0:64]
    d_b_in[...] = moved[32:33, 0:64]
    d_b_mid[...] = moved[40:41, 0:64]
    d_out[...] = moved[16:32, 0:64] * 0.25
    d_b_out[...] = (moved[48:64, :] * 0.25).T[0:1, :]


def pairs(value, axis, links):
    return lax.ppermute(value, axis, [(a, b) for a, b in links] + [(b, a) for a, b in links])


def swapped(even, odd, axis, count):
    far = pairs(odd, axis, [(i, i + 1) for i in range(1, count - 1, 2)])
    return pairs(even, axis, [(i, i + 1) for i in range(0, count - 1, 2)]), far


def params(mebibytes):
    return pltpu.CompilerParams(vmem_limit_bytes=mebibytes * 1024 * 1024)


def cost(flops, size):
    return pl.CostEstimate(flops=flops, bytes_accessed=size, transcendentals=0)


def solution(mesh):
    parts = Mesh(mesh.devices.reshape(4, 4, 4, 2, 2), ("zh", "y", "x", "c", "zl"))
    gx, gy, sa = ("zh", "y"), ("x", "c"), "zl"
    ring = ("zh", "zl")
    wide = P(sa, None, None, gx, gy)
    flat = P(sa, None, gx, gy)
    cells = 4194304
    far = pl.BlockSpec(memory_space=pltpu.HBM)
    shape = jax.ShapeDtypeStruct

    def local(moments, speed_x, flag_x, speed_y, flag_y, w_in, b_in, w_mid, b_mid, w_out, b_out, final_cot):
        mom = moments.reshape(2048, 128)
        cot = final_cot.reshape(2048, 128)
        sx, fx, sy, fy = (item.reshape(128, 128) for item in (speed_x, flag_x, speed_y, flag_y))
        b_in, b_mid, b_out = b_in.reshape(1, 64), b_mid.reshape(1, 64), b_out.reshape(1, 16)
        w_out = w_out.T
        s0, v0, speeds, x_even, x_odd, y_even, y_odd = pl.pallas_call(
            pack_kernel,
            in_specs=[far] * 12,
            out_shape=(
                shape((304, 1024), bf16), shape((256, 1024), f32), shape((512, 128), f32),
                shape((544, 128), bf16), shape((544, 128), bf16),
                shape((48, 768), f32), shape((48, 768), f32),
            ),
            scratch_shapes=[
                pltpu.VMEM((2048, 128), f32), pltpu.VMEM((2048, 128), bf16),
                pltpu.VMEM((128, 128), bf16), pltpu.VMEM((128, 128), jnp.int32),
                pltpu.VMEM((128, 128), bf16), pltpu.VMEM((128, 128), jnp.int32),
                pltpu.VMEM((16, 64), f32), pltpu.VMEM((1, 64), f32), pltpu.VMEM((64, 64), f32),
                pltpu.VMEM((1, 64), f32), pltpu.VMEM((16, 64), f32), pltpu.VMEM((1, 16), f32),
                pltpu.VMEM((2048, 128), f32), pltpu.VMEM((2, 544, 128), bf16),
                pltpu.VMEM((2, 8, 768), f32), pltpu.VMEM((128, 128), f32), pltpu.SemaphoreType.DMA((12,)),
            ],
            compiler_params=params(PACK),
            name="pack",
        )(cot, mom, sx, fx, sy, fy, w_in, b_in, w_mid, b_mid, w_out, b_out)
        x_even, x_odd = swapped(x_even, x_odd, gx, 16)
        y_even, y_odd = swapped(y_even, y_odd, gy, 8)
        ones_all, twos_all, base = pl.pallas_call(
            forward_kernel,
            out_shape=(shape((64, 16384), f32), shape((64, 16384), f32), shape((256, 1024), f32)),
            scratch_shapes=[pltpu.VMEM((128, 128), f32)],
            compiler_params=params(24),
            cost_estimate=cost(5000000000, 16000000),
            name="forward",
        )(s0)
        v1, coefs, grad_high, grad_low, x_even, x_odd, y_odd, sums = pl.pallas_call(
            main_kernel,
            out_shape=(
                shape((256, 1024), f32), shape((9 * 128, 128), f32),
                shape((64, 16384), bf16), shape((64, 16384), bf16),
                shape((256, 128), bf16), shape((256, 128), bf16),
                shape((16, 128), f32), shape((80, 128), f32),
            ),
            scratch_shapes=[
                pltpu.VMEM((256, 1024), f32),
                pltpu.VMEM((256, 1024), f32), pltpu.VMEM((256, 1024), bf16),
                pltpu.VMEM((112, 256), f32), pltpu.VMEM((2, 544, 128), bf16),
                pltpu.VMEM((2, 8, 768), f32), pltpu.VMEM((2, 256, 128), bf16),
                pltpu.VMEM((2, 8, 256), f32), pltpu.VMEM((128, 128), f32),
            ],
            compiler_params=params(32),
            cost_estimate=cost(15000000000, 40000000),
            name="network",
        )(
            ones_all, twos_all, base, s0, v0, speeds, x_odd, x_even, y_even, y_odd
        )
        y_even = pairs(sums, "c", [(0, 1)])
        sums = sums[0:64] + y_even[0:64]
        y_odd = pairs(jnp.concatenate([sums, y_odd], 0), gy, [(1, 2), (3, 4), (5, 6), (7, 0)])
        sums = sums + y_odd[0:64]
        steps = (
            (gy, [(0, 4), (1, 5), (2, 6), (3, 7)]),
            ("y", [(0, 1), (2, 3)]),
            ("y", [(0, 3), (1, 2)]),
            (ring, [(0, 1), (2, 3), (4, 5), (6, 7)]),
            (ring, [(1, 2), (3, 4), (5, 6), (7, 0)]),
        )
        places = {
            "x_even": (gx, x_even, [(i, i + 1) for i in range(0, 15, 2)]),
            "x_odd": (gx, x_odd, [(i, i + 1) for i in range(1, 15, 2)]),
        }
        beside = {0: ("x_even",), 2: ("x_odd",)}
        got = {}
        for index, (axis, links) in enumerate(steps):
            moving = {}
            for name in beside.get(index, ()):
                along, value, route = places[name]
                value, sums = lax.optimization_barrier((value, sums))
                moving[name] = pairs(value, along, route)
            if index == TAIL:
                v1, sums = lax.optimization_barrier((v1, sums))
                part = pl.pallas_call(
                    tail_kernel,
                    out_shape=shape((256, 1024), f32),
                    scratch_shapes=[pltpu.VMEM((128, 128), f32)],
                    compiler_params=params(16),
                    cost_estimate=cost(2000000000, 8000000),
                    name="tail",
                )(v1, coefs, grad_high, grad_low, s0)
            sums = sums + pairs(sums, axis, links)
            if index == TAIL:
                part, sums = lax.optimization_barrier((part, sums))
            if moving:
                names = list(moving)
                *values, sums = lax.optimization_barrier(tuple(moving[n] for n in names) + (sums,))
                got.update(zip(names, values))
        other = pairs(sums, ring, [(0, 3), (1, 6), (2, 5), (4, 7)])
        x_even, x_odd = got["x_even"], got["x_odd"]
        out = pl.pallas_call(
            finish_kernel,
            out_shape=shape((2048, 128), f32),
            scratch_shapes=[
                pltpu.VMEM((256, 1024), f32), pltpu.VMEM((2, 256, 128), bf16), pltpu.VMEM((2, 8, 256), f32)
            ],
            compiler_params=params(16),
            cost_estimate=cost(10000000, 6000000),
            name="finish",
        )(part, coefs, x_even, x_odd, y_even, y_odd)

        d_in, d_b_in, d_mid, d_b_mid, d_out, d_b_out = pl.pallas_call(
            lambda *refs: weights_kernel(1.0 / cells, *refs),
            out_shape=(
                shape((16, 64), f32), shape((1, 64), f32), shape((64, 64), f32),
                shape((1, 64), f32), shape((16, 64), f32), shape((1, 16), f32),
            ),
            compiler_params=params(16),
            name="weights",
        )(sums, other)
        return (
            out.reshape(final_cot.shape), d_in, d_b_in.reshape(64), d_mid, d_b_mid.reshape(64),
            d_out.T, d_b_out.reshape(16),
        )

    return jax.shard_map(
        local,
        mesh=parts,
        in_specs=(wide, flat, flat, flat, flat, P(), P(), P(), P(), P(), P(), wide),
        out_specs=(wide, P(), P(), P(), P(), P(), P()),
        check_vma=False,
    )
```
